256 devices in a mesh: frame: 64 (over y, z, x_lo), mp: 4 (over x_hi, core).
Axes of the slice: x: 4 (x_hi: 2, x_lo: 2; x = x_hi * 2 + x_lo), y: 4, z: 8, core: 2. Of those that a mesh axis runs over, the one named last changes fastest.
Arguments:
- latents: bfloat16 [512, 96, 3072], P(('frame', 'mp')), may hold values from -6 to 6
- levels: int32 [64], P('frame'), may hold values from 0 to 49, as said below
- window_reach: int32 [64], P('frame'), may hold values from 1 to 2, as said below
- query_gain: float32 [128], replicated, may hold values from 1.2 to 5
- key_gain: float32 [128], replicated, may hold values from 1.2 to 5
- qkv_weight: bfloat16 [3072, 4608], P('mp'), may hold values from -0.109375 to 0.109375
- out_weight: bfloat16 [1536, 3072], P('mp'), may hold values from -0.15625 to 0.15625
- mod_weight: bfloat16 [256, 9216], P(None, 'mp'), may hold values from -0.375 to 0.375
Outputs:
- queue_next: bfloat16 [512, 96, 3072], P(('frame', 'mp'))
- velocity: bfloat16 [512, 96, 3072], P(('frame', 'mp'))
The draws below stay inside these ranges and needn't reach their ends.
Inputs may be any that keep to these rules, and one draw needn't show every extreme that they name: `levels`: some slot has level 49 and some has 0. `window_reach`: some slot has reach 2 and some has 1.
All inputs are finite; a program needn't handle non-finite values.
Results may differ from the reference program's by a relative error of at most 0.027.
Values may be sent and summed in bfloat16 or wider, within the bound.
A program may use at most 128 MiB of HBM per device.

```python
import math
import jax
import jax.numpy as jnp
from jax import lax

D = 3072
HEADS = 12
HEAD = 128
FREQ = 256
NOISE_LEVELS = 50
REACH_LIMIT = 2
SPATIAL = 96
QUEUE_SLOTS = 64
FRAMES = 512


def draw_levels(key, part):
    key = jax.random.fold_in(key, 11)
    leading_item, trailing_item = jax.random.split(key)
    sampled_values = jax.random.randint(leading_item, (QUEUE_SLOTS,), 0, NOISE_LEVELS)
    sorted_order = jax.random.permutation(trailing_item, QUEUE_SLOTS)
    sampled_values = sampled_values.at[sorted_order[0]].set(NOISE_LEVELS - 1).at[sorted_order[1]].set(0)
    return sampled_values.astype(jnp.int32)


def draw_window_reach(key, part):
    key = jax.random.fold_in(key, 17)
    leading_item, trailing_item = jax.random.split(key)
    sampled_values = jax.random.randint(leading_item, (QUEUE_SLOTS,), 1, REACH_LIMIT + 1)
    sorted_order = jax.random.permutation(trailing_item, QUEUE_SLOTS)
    sampled_values = sampled_values.at[sorted_order[0]].set(REACH_LIMIT).at[sorted_order[1]].set(1)
    return sampled_values.astype(jnp.int32)


def draw_query_gain(key, part):
    key = jax.random.fold_in(key, 31)
    return jax.random.uniform(key, (HEAD,), jnp.float32, 1.2, 2.5)


def draw_key_gain(key, part):
    key = jax.random.fold_in(key, 37)
    return jax.random.uniform(key, (HEAD,), jnp.float32, 1.2, 2.5)


def level_of(own_key, dims, cuts, smallest, top_value):
    factor_of = 1.0
    for dim, parts in cuts:
        draws = jax.random.uniform(jax.random.fold_in(jax.random.fold_in(own_key, 6), dim), (parts,), jnp.float32, smallest / len(cuts), top_value / len(cuts))
        factor_of = factor_of * jnp.repeat(jnp.exp(draws), dims[dim] // parts).reshape((-1,) + (1,) * (len(dims) - 1 - dim))
    return factor_of


def bell_draw(rng, shape, deviation, bound, pieces=(), kind=jnp.bfloat16):
    array = deviation * jax.random.normal(rng, shape, jnp.float32)
    if pieces:
        array = array * level_of(rng, shape, pieces, -0.22, 0.18)
    return jnp.clip(array, -bound, bound).astype(kind)


def setup_inputs(seed: int = 0) -> dict:
    streams_of = jax.random.split(jax.random.key(seed), 9)
    latents = bell_draw(streams_of[0], (FRAMES, SPATIAL, D), 1.0, 6.0, ((0, 256),))
    levels = draw_levels(jax.random.fold_in(streams_of[8], 71), 0)
    window_reach = draw_window_reach(jax.random.fold_in(streams_of[8], 71), 0)
    query_gain = draw_query_gain(jax.random.fold_in(streams_of[8], 71), 0)
    key_gain = draw_key_gain(jax.random.fold_in(streams_of[8], 71), 0)
    qkv_weight = bell_draw(streams_of[5], (D, 3 * HEADS * HEAD), D ** -0.5, 0.109375, ((0, 4),))
    out_weight = bell_draw(streams_of[6], (HEADS * HEAD, D), (HEADS * HEAD) ** -0.5, 0.15625, ((0, 4),))
    mod_weight = bell_draw(streams_of[7], (FREQ, 3 * D), FREQ ** -0.5, 0.375, ((1, 4),))
    return dict(latents=latents, levels=levels, window_reach=window_reach, query_gain=query_gain, key_gain=key_gain, qkv_weight=qkv_weight, out_weight=out_weight, mod_weight=mod_weight)


flow_shift = 7.0

def flow_sigma(position):
    return flow_shift * position / (1.0 + (flow_shift - 1.0) * position)

def level_terms(level_value):
    upper = (level_value + 1.0) / NOISE_LEVELS
    lower = level_value / NOISE_LEVELS
    sigma_now = flow_sigma(upper)
    step_size = sigma_now - flow_sigma(lower)
    half_count = FREQ // 2
    index_row = jnp.arange(half_count).astype(jnp.float32)
    frequency = jnp.exp(-math.log(10000.0) * index_row / half_count)
    angles = 1000.0 * sigma_now[:, None] * frequency[None, :]
    embedded = jnp.concatenate([jnp.cos(angles), jnp.sin(angles)], axis=-1)
    return (jax.nn.silu(embedded).astype(jnp.bfloat16), step_size)

def head_norm(values, gain):
    widened = values.astype(jnp.float32)
    meansq = lax.optimization_barrier(jnp.mean(widened * widened, axis=-1, keepdims=True))
    return (widened * lax.rsqrt(meansq + 1e-06) * gain).astype(jnp.bfloat16)

def modulate(token_rows, shift_row, scale_row):
    widened = token_rows.astype(jnp.float32)
    center = lax.optimization_barrier(jnp.mean(widened, axis=-1, keepdims=True))
    spread = lax.optimization_barrier(jnp.mean((widened - center) * (widened - center), axis=-1, keepdims=True))
    normed = (widened - center) * lax.rsqrt(spread + 1e-06)
    return (normed * (1.0 + scale_row) + shift_row).astype(jnp.bfloat16)

def reference(latents, levels, window_reach, query_gain, key_gain, qkv_weight, out_weight, mod_weight):
    slot_count = levels.shape[0]
    total_frames, spatial, width = latents.shape
    group = total_frames // slot_count
    inner = out_weight.shape[0]
    heads = inner // HEAD
    activity, step_sizes = level_terms(levels.astype(jnp.float32))
    modulation = jnp.dot(activity, mod_weight, preferred_element_type=jnp.float32)
    slot_rows = latents.reshape(slot_count, group * spatial, width)

    def project(pack):
        token_rows, shift_row, scale_row = pack
        hidden = modulate(token_rows, shift_row, scale_row)
        projected = jnp.dot(hidden, qkv_weight, preferred_element_type=jnp.float32).astype(jnp.bfloat16)
        queries = head_norm(projected[:, :inner].reshape(-1, heads, HEAD), query_gain)
        keys = head_norm(projected[:, inner:2 * inner].reshape(-1, heads, HEAD), key_gain)
        return (queries, keys.reshape(-1, inner), projected[:, 2 * inner:])
    queries, keys, values = lax.map(project, (slot_rows, modulation[:, :width], modulation[:, width:2 * width]))
    padded_keys = jnp.pad(keys.reshape(total_frames, spatial, inner), ((REACH_LIMIT, REACH_LIMIT), (0, 0), (0, 0)))
    padded_values = jnp.pad(values.reshape(total_frames, spatial, inner), ((REACH_LIMIT, REACH_LIMIT), (0, 0), (0, 0)))

    def attend(pack):
        slot, token_rows, query_rows, gate_row, step_size, reach_value = pack
        start = (slot * group).astype(jnp.int32)
        span = group + 2 * REACH_LIMIT
        key_block = lax.dynamic_slice_in_dim(padded_keys, start, span, 0).reshape(-1, heads, HEAD)
        value_block = lax.dynamic_slice_in_dim(padded_values, start, span, 0).reshape(-1, heads, HEAD)
        query_frame = start + jnp.arange(group * spatial, dtype=jnp.int32) // spatial
        key_frame = start - REACH_LIMIT + jnp.arange(span * spatial, dtype=jnp.int32) // spatial
        valid = jnp.abs(key_frame[None, :] - query_frame[:, None]) <= reach_value
        valid = valid & (key_frame >= 0)[None, :] & (key_frame < total_frames)[None, :]
        scores = jnp.einsum('qhd,khd->hqk', query_rows.astype(jnp.float32), key_block.astype(jnp.float32)) / math.sqrt(HEAD)
        scores = jnp.where(valid[None], scores, -jnp.inf)
        peak = lax.optimization_barrier(jnp.max(scores, axis=-1, keepdims=True))
        raised = jnp.where(valid[None], jnp.exp(scores - peak), 0.0)
        weights = (raised / lax.optimization_barrier(jnp.sum(raised, axis=-1, keepdims=True))).astype(jnp.bfloat16)
        mixed = jnp.einsum('hqk,khd->qhd', weights.astype(jnp.float32), value_block.astype(jnp.float32))
        mixed = mixed.astype(jnp.bfloat16).reshape(-1, inner)
        attended = jnp.dot(mixed, out_weight, preferred_element_type=jnp.float32)
        base = token_rows.astype(jnp.float32)
        velocity_full = base + gate_row * attended
        stepped = (base - step_size * velocity_full).astype(jnp.bfloat16)
        return (velocity_full.astype(jnp.bfloat16), stepped)
    slot_ids = jnp.arange(slot_count, dtype=jnp.int32)
    velocity, stepped = lax.map(attend, (slot_ids, slot_rows, queries, modulation[:, 2 * width:], step_sizes, window_reach))
    queue_next = jnp.roll(stepped.reshape(latents.shape), -group, axis=0)
    return (queue_next, velocity.reshape(latents.shape))
```

```python
import functools
import math

import jax
import jax.numpy as jnp
from jax import lax
from jax.experimental import pallas as pl
from jax.experimental.pallas import tpu as pltpu
from jax.sharding import PartitionSpec as P

D = 3072
HEADS = 12
HEAD = 128
FREQ = 256
NOISE_LEVELS = 50
REACH_LIMIT = 2
SPATIAL = 96
FRAMES = 512
INNER = HEADS * HEAD
ROWS = 2 * SPATIAL
CHIP = 2 * ROWS
HALF = INNER // 2
PAIR = 2 * HEAD
WINDOW = (2 * REACH_LIMIT + 1) * SPATIAL
ROUNDS = 3
NY, NZ = 4, 8
MESH = pl.DeviceIdType.MESH
F32 = jnp.float32
BF16 = jnp.bfloat16

flow_shift = 7.0


def flow_sigma(position):
    return flow_shift * position / (1.0 + (flow_shift - 1.0) * position)


def level_terms(level_value):
    upper = (level_value + 1.0) / NOISE_LEVELS
    lower = level_value / NOISE_LEVELS
    sigma_now = flow_sigma(upper)
    step_size = sigma_now - flow_sigma(lower)
    half_count = FREQ // 2
    index_row = jnp.arange(half_count).astype(F32)
    frequency = jnp.exp(-math.log(10000.0) * index_row / half_count)
    angles = 1000.0 * sigma_now[:, None] * frequency[None, :]
    embedded = jnp.concatenate([jnp.cos(angles), jnp.sin(angles)], axis=-1)
    return (jax.nn.silu(embedded).astype(BF16), step_size)


HOPS = {
    ("z", "a", 1): 4, ("z", "a", -1): 3, ("z", "b", 1): 3, ("z", "b", -1): 4,
    ("y", "a", 1): 2, ("y", "a", -1): 1, ("y", "b", 1): 1, ("y", "b", -1): 2,
}


def kernel(
    x_hbm, w_hbm, wo_hbm, modpart, step, bias, qgain, kgain,
    vel_hbm, next_hbm,
    weights, out_weights, hidden, own_x, other_x, mod, shift, scale, gate,
    queries, keys, values, mixed, vel, stepped, send_sem, recv_sem, local_sem, mod_sem,
):
    f = lax.axis_index("frame")
    m = lax.axis_index("mp")
    xl = f % 2
    z = (f // 2) % NZ
    y = f // (2 * NZ)
    xh = m // 2
    c = m % 2

    def frame_of(yy, zz, ll):
        return (yy * NZ + zz) * 2 + ll

    twin = (f, xh * 2 + 1 - c)
    inner = (frame_of(y, z, 1 - xl), m)
    cross = [(frame_of(y, z, 1 - xl), (1 - xh) * 2 + core) for core in range(2)]
    ring = {
        ("z", 1): (frame_of(y, (z + 1) % NZ, xl), m),
        ("z", -1): (frame_of(y, (z + NZ - 1) % NZ, xl), m),
        ("y", 1): (frame_of((y + 1) % NY, z, xl), m),
        ("y", -1): (frame_of((y + NY - 1) % NY, z, xl), m),
    }
    group = [(f, (m + i) % 4) for i in range(1, 4)]
    count = 64
    before = [((f + count - 1) % count, xh * 2 + core) for core in range(2)]
    after = [((f + 1) % count, xh * 2 + core) for core in range(2)]
    chip_before = (f + count - 1 + xh) % count
    chip_after = (f + xh) % count
    halo = [(chip, (1 - xh) * 2 + core) for chip in (chip_before, chip_after) for core in range(2)]

    started = []
    numbers = {}

    def number(key):
        return numbers.setdefault(key, len(numbers))

    def remote(src, dst, key, device, keep=True):
        copy = pltpu.make_async_remote_copy(
            src_ref=src, dst_ref=dst, send_sem=send_sem.at[len(started) if keep else 0],
            recv_sem=recv_sem.at[key if not isinstance(key, tuple) else number(key)],
            device_id=device, device_id_type=MESH,
        )
        return copy

    def send(src, dst, key, device):
        copy = remote(src, dst, key, device)
        started.append(copy)
        copy.start()

    def received(dst, key):
        remote(dst, dst, key, twin, keep=False).wait_recv()

    locals_started = {}

    def load(src, dst, key, place):
        copy = pltpu.make_async_copy(src, dst, local_sem.at[place])
        copy.start()
        locals_started.setdefault(key, []).append(copy)

    load(x_hbm, own_x, "x", 0)
    for r in range(ROUNDS):
        for part in range(3):
            load(
                w_hbm.at[:, pl.ds(pl.multiple_of(part * INNER + c * HALF + r * PAIR, PAIR), PAIR)],
                weights.at[r, pl.ds(pl.multiple_of(m * 768, 768), 768), pl.ds(part * PAIR, PAIR)],
                r, 1 + r * 3 + part,
            )
    load(
        wo_hbm.at[:, pl.ds(pl.multiple_of(c * INNER, INNER), INNER)],
        out_weights.at[pl.ds(pl.multiple_of(m * 384, 384), 384)],
        ROUNDS, 1 + ROUNDS * 3,
    )
    mod[m] = modpart[...]

    barrier = pltpu.get_barrier_semaphore()
    greeted = [twin, inner, *cross, *ring.values(), *group[1:2], *before, *after, *halo]
    for device in greeted + [group[0], group[2]]:
        pl.semaphore_signal(barrier, inc=1, device_id=device, device_id_type=MESH)
    pl.semaphore_wait(barrier, len(greeted) + 2)

    buffers = [weights.at[r] for r in range(ROUNDS)] + [out_weights]
    shard = [768] * ROUNDS + [384]
    size = {"z": [48] * ROUNDS + [16], "y": [96] * ROUNDS + [64]}
    base = {"z": [0] * 4, "y": [384] * ROUNDS + [128]}
    own = {"z": z, "y": y}
    length = {"z": NZ, "y": NY}
    missing = (1 - xh) * 2
    shard_of = {"a": missing + xl, "b": missing + 1 - xl}

    def piece(axis, owner_shard, j, r):
        rows = size[axis][r]
        start = owner_shard * shard[r] + base[axis][r] + j * rows
        return buffers[r].at[pl.ds(pl.multiple_of(start, 16), rows)]

    fetched = []

    def fetch(r):
        first = len(started)

        @pl.when(c == 1 - xl)
        def _():
            for axis in ("z", "y"):
                rows = size[axis][r]
                here = pl.ds(pl.multiple_of(base[axis][r] + own[axis] * rows, 16), rows)
                there = pl.ds(
                    pl.multiple_of(m * shard[r] + base[axis][r] + own[axis] * rows, 16), rows
                )
                for core in range(2):
                    if r < ROUNDS:
                        for part in range(3):
                            send(
                                w_hbm.at[here, pl.ds(part * INNER + core * HALF + r * PAIR, PAIR)],
                                weights.at[r, there, pl.ds(part * PAIR, PAIR)],
                                ("fetch", axis, r), cross[core],
                            )
                    else:
                        send(
                            wo_hbm.at[here, pl.ds(core * INNER, INNER)],
                            out_weights.at[there],
                            ("fetch", axis, r), cross[core],
                        )

        for i in range(first, len(started)):
            rows = size["z" if i - first < (len(started) - first) // 2 else "y"][r]
            columns = pl.ds(0, PAIR if r < ROUNDS else INNER)
            source = (w_hbm if r < ROUNDS else wo_hbm).at[pl.ds(0, rows), columns]
            started[i] = None
            fetched.append((source, buffers[r].at[pl.ds(0, rows), columns], i))

    def exchange(r):
        if r < ROUNDS:
            for part in range(3):
                send(
                    w_hbm.at[:, pl.ds(pl.multiple_of(part * INNER + (1 - c) * HALF + r * PAIR, PAIR), PAIR)],
                    weights.at[r, pl.ds(pl.multiple_of(m * 768, 768), 768), pl.ds(part * PAIR, PAIR)],
                    ("twin", r), twin,
                )
        else:
            send(
                wo_hbm.at[:, pl.ds(pl.multiple_of((1 - c) * INNER, INNER), INNER)],
                out_weights.at[pl.ds(pl.multiple_of(m * 384, 384), 384)],
                ("twin", r), twin,
            )

    def ring_send(axis, way, half, k, r):
        if k >= HOPS[axis, half, way]:
            return
        j = (own[axis] - way * k + length[axis]) % length[axis]
        region = piece(axis, shard_of[half], j, r)
        send(region, region, (axis, way, half, k + 1, r), ring[axis, way])

    def ring_step(axis, half, k, r):
        for way in (1, -1):
            if k <= HOPS[axis, half, way]:
                j = (own[axis] - way * k + length[axis]) % length[axis]
                received(piece(axis, shard_of[half], j, r), (axis, way, half, k, r))
                ring_send(axis, way, half, k, r)

    def event(r, k):
        if k == 1:
            for axis in ("z", "y"):
                region = piece(axis, shard_of["a"], own[axis], r)
                received(region, ("fetch", axis, r))
                send(region, region, ("swap", axis, r), inner)
                for way in (1, -1):
                    ring_send(axis, way, "a", 0, r)
        elif k == 2:
            for axis in ("z", "y"):
                received(piece(axis, shard_of["b"], own[axis], r), ("swap", axis, r))
                for way in (1, -1):
                    ring_send(axis, way, "b", 0, r)
        else:
            steps = {
                3: [("z", "a", 1)], 4: [("z", "b", 1)], 5: [("z", "a", 2), ("y", "a", 1)],
                6: [("z", "b", 2)], 7: [("z", "a", 3), ("y", "b", 1)], 8: [("z", "b", 3)],
                9: [("z", "a", 4), ("z", "b", 4), ("y", "a", 2), ("y", "b", 2)],
            }[k]
            for axis, half, hop in steps:
                ring_step(axis, half, hop, r)

    def complete(r):
        for copy in locals_started.pop(r):
            copy.wait()
        rows = shard[r]
        start = (xh * 2 + 1 - c) * rows
        received(buffers[r].at[pl.ds(pl.multiple_of(start, rows), rows)], ("twin", r))

    for device in group:
        send(modpart, mod.at[m], mod_sem_key + m, device)
    fetch(0)
    exchange(0)
    send(
        x_hbm.at[:, pl.ds(pl.multiple_of((1 - c) * INNER, INNER), INNER)], other_x, ("x",), twin
    )
    for i in range(1, 4):
        source = (m + i) % 4
        received(mod.at[source], mod_sem_key + source)
    shift[:, :2304] = mod[0]
    shift[:, 2304:] = mod[1, :, :768]
    scale[:, :1536] = 1.0 + mod[1, :, 768:]
    scale[:, 1536:] = 1.0 + mod[2, :, :1536]
    gate[:, :768] = mod[2, :, 1536:]
    gate[:, 768:] = mod[3]
    for copy in locals_started.pop("x"):
        copy.wait()

    own_rows = pl.multiple_of(c * ROWS, ROWS)

    @pl.loop(0, ROWS // 16)
    def _(i):
        rows = own_x[pl.ds(pl.multiple_of(i * 16, 16), 16), :].astype(F32)
        center = jnp.mean(rows, axis=-1, keepdims=True)
        rows = rows - center
        spread = jnp.mean(rows * rows, axis=-1, keepdims=True)
        out = rows * lax.rsqrt(spread + 1e-06) * scale[...] + shift[...]
        hidden[pl.ds(pl.multiple_of(own_rows + i * 16, 16), 16), :] = out.astype(BF16)

    mine = hidden.at[pl.ds(own_rows, ROWS)]
    send(mine, mine, ("hidden",), twin)
    halo_chip = jnp.where(c == 1, chip_after, chip_before)
    halo_base = jnp.where(c == 1, CHIP, CHIP + ROWS)
    for core in range(2):
        send(
            hidden.at[pl.ds(pl.multiple_of(own_rows + core * SPATIAL, 16), SPATIAL)],
            hidden.at[pl.ds(pl.multiple_of(halo_base + core * SPATIAL, 16), SPATIAL)],
            halo_key + 1 - c, (halo_chip, (1 - xh) * 2 + core),
        )

    def halo_forward():
        for side in range(2):
            region = hidden.at[
                pl.ds(pl.multiple_of(CHIP + side * ROWS + c * SPATIAL, 16), SPATIAL)
            ]
            received(region, halo_key + side)
            send(region, region, ("forward", side), twin)

    def halo_arrived():
        for side in range(2):
            region = hidden.at[
                pl.ds(pl.multiple_of(CHIP + side * ROWS + (1 - c) * SPATIAL, 16), SPATIAL)
            ]
            received(region, ("forward", side))

    def product(lo, r, part):
        return jnp.dot(
            hidden[lo : lo + CHIP, :], weights[r, :, part * PAIR : (part + 1) * PAIR],
            preferred_element_type=F32,
        )

    def normed(tile, gain):
        return tile * lax.rsqrt(jnp.mean(tile * tile, axis=-1, keepdims=True) + 1e-06) * gain

    def project(r, part, own_part):
        tile = product(0 if own_part else CHIP, r, part)
        for h in range(2):
            columns = slice(h * HEAD, (h + 1) * HEAD)
            head = tile[:, columns]
            if part == 0:
                head = normed(head, qgain[...])
            elif part == 1:
                head = normed(head, kgain[...])
            head = head.astype(BF16)
            if part == 0:
                queries[r, :, columns] = head
            else:
                target = keys if part == 1 else values
                if own_part:
                    target[r, ROWS : ROWS + CHIP, columns] = head
                else:
                    target[r, 0:ROWS, columns] = head[:ROWS]
                    target[r, ROWS + CHIP :, columns] = head[ROWS:]

    def attend(r):
        @pl.loop(0, 4)
        def _(i):
            q_rows = pl.ds(pl.multiple_of(i * SPATIAL, 16), SPATIAL)
            k_rows = pl.ds(pl.multiple_of(i * SPATIAL, 16), WINDOW)
            for h in range(2):
                columns = slice(h * HEAD, (h + 1) * HEAD)
                scores = lax.dot_general(
                    queries[r, q_rows, columns], keys[r, k_rows, columns],
                    (((1,), (1,)), ((), ())), preferred_element_type=F32,
                ) + bias[i]
                peak = jnp.max(scores, axis=-1, keepdims=True)
                raised = jnp.exp(scores - peak)
                total = jnp.sum(raised, axis=-1, keepdims=True)
                out = jnp.dot(
                    raised.astype(BF16), values[r, k_rows, columns], preferred_element_type=F32
                )
                place = pl.multiple_of(c * HALF + r * PAIR + h * HEAD, HEAD)
                mixed[q_rows, pl.ds(place, HEAD)] = (out / total).astype(BF16)

        region = mixed.at[:, pl.ds(pl.multiple_of(c * HALF + r * PAIR, PAIR), PAIR)]
        send(region, region, ("mixed", r), twin)

    work = {
        9: [lambda: complete(0), lambda: project(0, 0, True)],
        10: [lambda: project(0, 1, True)],
        11: [lambda: project(0, 2, True)],
        15: [lambda: complete(1), lambda: project(1, 0, True)],
        16: [lambda: project(1, 1, True)],
        17: [halo_forward, lambda: project(1, 2, True)],
        18: [halo_arrived, lambda: project(0, 1, False)],
        19: [lambda: project(0, 2, False), lambda: attend(0)],
        20: [lambda: project(1, 1, False), lambda: project(1, 2, False)],
        21: [lambda: attend(1)],
        22: [lambda: complete(2), lambda: project(2, 0, True)],
        23: [lambda: project(2, 1, True), lambda: project(2, 1, False)],
        24: [lambda: project(2, 2, True), lambda: project(2, 2, False)],
        25: [lambda: attend(2)],
    }
    received_hidden = False
    for tick in range(1, 28):
        for r in range(4):
            k = tick - 6 * r
            if 1 <= k <= 9:
                event(r, k)
            if k == 2 and r < 3:
                fetch(r + 1)
                exchange(r + 1)
        if tick == 9 and not received_hidden:
            other = hidden.at[pl.ds(pl.multiple_of((1 - c) * ROWS, ROWS), ROWS)]
            received(other, ("hidden",))
            received_hidden = True
        for item in work.get(tick, []):
            item()
    complete(3)
    for r in range(ROUNDS):
        region = mixed.at[:, pl.ds(pl.multiple_of((1 - c) * HALF + r * PAIR, PAIR), PAIR)]
        received(region, ("mixed", r))
    received(other_x, ("x",))

    half_columns = pl.multiple_of(c * INNER, INNER)
    step_row = step[...]
    groups = 3
    wide = INNER // groups
    finals = []
    for g in range(groups):
        for t in range(2):
            lo = g * wide + t * PAIR
            attended = jnp.dot(
                mixed[...], out_weights[:, lo : lo + PAIR], preferred_element_type=F32
            )
            gate_row = gate[:, pl.ds(pl.multiple_of(half_columns + lo, PAIR), PAIR)]
            mine_x = own_x[:, pl.ds(pl.multiple_of(half_columns + lo, PAIR), PAIR)].astype(F32)
            twin_x = other_x[:, lo : lo + PAIR].astype(F32)
            for base_x, at in ((mine_x, own_rows), (twin_x, ROWS - own_rows)):
                at = pl.multiple_of(at, ROWS)
                stage = pl.ds(at, ROWS)
                vel[stage, lo : lo + PAIR] = base_x.astype(BF16)
            base_x = vel[:, lo : lo + PAIR].astype(F32)
            full = base_x + gate_row * attended
            vel[:, lo : lo + PAIR] = full.astype(BF16)
            stepped[:, lo : lo + PAIR] = (base_x - step_row * full).astype(BF16)
        columns = pl.ds(pl.multiple_of(half_columns + g * wide, wide), wide)
        stage_columns = pl.ds(g * wide, wide)
        for core in range(2):
            send(
                stepped.at[pl.ds(core * ROWS, ROWS), stage_columns],
                next_hbm.at[:, columns], next_key + 2 * g + c, before[core],
            )
        twin_rows = pl.ds(pl.multiple_of((1 - c) * ROWS, ROWS), ROWS)
        send(
            vel.at[twin_rows, stage_columns], vel_hbm.at[:, columns], ("velocity", g), twin
        )
        copy = pltpu.make_async_copy(
            vel.at[pl.ds(own_rows, ROWS), stage_columns], vel_hbm.at[:, columns],
            local_sem.at[11 + g],
        )
        copy.start()
        finals.append(copy)
    for g in range(groups):
        for core in range(2):
            received(next_hbm.at[:, pl.ds(core * INNER + g * wide, wide)], next_key + 2 * g + core)
        columns = pl.ds(pl.multiple_of((1 - c) * INNER + g * wide, wide), wide)
        received(vel_hbm.at[:, columns], ("velocity", g))
    for copy in finals:
        copy.wait()
    assert len(started) <= SENDS and len(numbers) <= mod_sem_key
    for copy in started:
        if copy is not None:
            copy.wait_send()

    @pl.when(c == 1 - xl)
    def _():
        for src, dst, i in fetched:
            pltpu.make_async_remote_copy(
                src_ref=src, dst_ref=dst, send_sem=send_sem.at[i], recv_sem=recv_sem.at[0],
                device_id=twin, device_id_type=MESH,
            ).wait_send()


mod_sem_key = 160
halo_key = 164
next_key = 166
SEMAPHORES = 172
SENDS = 256


def per_device(
    latents, levels, window_reach, query_gain, key_gain, qkv_weight, out_weight, mod_weight
):
    activity, step_size = level_terms(levels.astype(F32))
    own_part = jnp.dot(activity, mod_weight, preferred_element_type=F32)
    f = lax.axis_index("frame")
    first = f * 8 + (lax.axis_index("mp") // 2) * 4
    offset = jnp.arange(WINDOW, dtype=jnp.int32) // SPATIAL - REACH_LIMIT
    key_frame = first + jnp.arange(4, dtype=jnp.int32)[:, None] + offset[None, :]
    valid = (jnp.abs(offset)[None, :] <= window_reach[0]) & (key_frame >= 0) & (key_frame < FRAMES)
    bias = jnp.where(valid, 0.0, -1e30).astype(F32).reshape(4, 1, WINDOW)
    step_row = jnp.broadcast_to(step_size.reshape(1, 1), (1, PAIR))
    vmem = pl.BlockSpec(memory_space=pltpu.VMEM)
    hbm = pl.BlockSpec(memory_space=pl.ANY)
    shape = jax.ShapeDtypeStruct((ROWS, D), BF16)
    velocity, queue_next = pl.pallas_call(
        kernel,
        out_shape=(shape, shape),
        in_specs=[hbm, hbm, hbm, vmem, vmem, vmem, vmem, vmem],
        out_specs=(hbm, hbm),
        scratch_shapes=[
            pltpu.VMEM((ROUNDS, D, 3 * PAIR), BF16),
            pltpu.VMEM((INNER, INNER), BF16),
            pltpu.VMEM((2 * CHIP, D), BF16),
            pltpu.VMEM((ROWS, D), BF16),
            pltpu.VMEM((ROWS, INNER), BF16),
            pltpu.VMEM((4, 1, 2304), F32),
            pltpu.VMEM((1, D), F32),
            pltpu.VMEM((1, D), F32),
            pltpu.VMEM((1, D), F32),
            pltpu.VMEM((ROUNDS, CHIP, PAIR), BF16),
            pltpu.VMEM((ROUNDS, 2 * CHIP, PAIR), BF16),
            pltpu.VMEM((ROUNDS, 2 * CHIP, PAIR), BF16),
            pltpu.VMEM((CHIP, INNER), BF16),
            pltpu.VMEM((CHIP, INNER), BF16),
            pltpu.VMEM((CHIP, INNER), BF16),
            pltpu.SemaphoreType.DMA((SENDS,)),
            pltpu.SemaphoreType.DMA((SEMAPHORES,)),
            pltpu.SemaphoreType.DMA((16,)),
            pltpu.SemaphoreType.DMA((1,)),
        ],
        compiler_params=pltpu.CompilerParams(
            collective_id=0, has_side_effects=True, vmem_limit_bytes=56 * 2**20
        ),
    )(
        latents.reshape(ROWS, D), qkv_weight, out_weight, own_part, step_row, bias,
        (query_gain / math.sqrt(HEAD)).reshape(1, HEAD), key_gain.reshape(1, HEAD),
    )
    return (queue_next.reshape(2, SPATIAL, D), velocity.reshape(2, SPATIAL, D))


def solution(mesh):
    return jax.shard_map(
        per_device,
        mesh=mesh,
        in_specs=(
            P(("frame", "mp"), None, None),
            P("frame"),
            P("frame"),
            P(),
            P(),
            P("mp", None),
            P("mp", None),
            P(None, "mp"),
        ),
        out_specs=(P(("frame", "mp"), None, None), P(("frame", "mp"), None, None)),
        check_vma=False,
    )
```

```python
import heapq
import math

import jax
import jax.numpy as jnp
from jax import lax
from jax.experimental import pallas as pl
from jax.experimental.pallas import tpu as pltpu
from jax.sharding import PartitionSpec as P

D = 3072
HEADS = 12
HEAD = 128
FREQ = 256
NOISE_LEVELS = 50
REACH_LIMIT = 2
SPATIAL = 96
FRAMES = 512
INNER = HEADS * HEAD
ROWS = 2 * SPATIAL
CHIP = 2 * ROWS
HALF = INNER // 2
PAIR = 2 * HEAD
WINDOW = (2 * REACH_LIMIT + 1) * SPATIAL
ROUNDS = 3
NY, NZ = 4, 8
MESH = pl.DeviceIdType.MESH
F32 = jnp.float32
BF16 = jnp.bfloat16

flow_shift = 7.0


def flow_sigma(position):
    return flow_shift * position / (1.0 + (flow_shift - 1.0) * position)


HOPS = {
    ("z", "a", 1): 4, ("z", "a", -1): 3, ("z", "b", 1): 3, ("z", "b", -1): 4,
    ("y", "a", 1): 2, ("y", "a", -1): 1, ("y", "b", 1): 1, ("y", "b", -1): 2,
}
SHARD = [768] * ROUNDS + [384] * 2
PIECE = {"z": [48] * ROUNDS + [0] * 2, "y": [96] * ROUNDS + [96] * 2}
BASE = {"z": [0] * 5, "y": [384] * ROUNDS + [0] * 2}
AXES = [[axis for axis in "zy" if PIECE[axis][r]] for r in range(5)]
WIDE = 3 * PAIR


def plan():
    rate, latency, backlog, halo_time = 46500.0, 2.2, 2.2, 25.0
    busy, ready, arrivals, actions, work, waiting = {}, {}, [], [], [], []

    def cost(axis, r):
        return PIECE[axis][r] * WIDE * 2 / rate

    def transmit(link, time, length, what):
        busy[link] = max(busy.get(link, 0.0), time) + length
        heapq.heappush(arrivals, (busy[link] + latency, len(actions), len(arrivals), what))

    def offer(axis, way, half, k, r):
        rest = HOPS[axis, half, way] - k
        if rest > 0:
            item = (r, -rest, len(actions), ("ring", axis, way, half, k, r))
            ready.setdefault((axis, way), []).append(item)

    left = [0] * 5
    for r in range(5):
        for axis in AXES[r]:
            left[r] += 2 + sum(hops for key, hops in HOPS.items() if key[0] == axis)
            transmit("cross", 0.0, cost(axis, r), ("fetch", axis, r))
    swaps = sum(len(axes) for axes in AXES)
    now = 6.0
    transmit("cross", now, halo_time, ("halo",))
    halo = False

    def halo_work(r):
        return [("project", r, 1, False), ("project", r, 2, False), ("attend", r)]

    while True:
        if arrivals and arrivals[0][0] <= now:
            what = heapq.heappop(arrivals)[-1]
            actions.append(("wait", *what))
            now += 0.05
            if what[0] == "halo":
                halo = True
                work.append(("halo",))
                for r in waiting:
                    work.extend(halo_work(r))
                continue
            r = what[-1]
            left[r] -= 1
            if what[0] == "fetch":
                ready.setdefault("inner", []).append((r, 0, len(actions), ("swap", what[1], r)))
            if what[0] == "ring":
                offer(*what[1:])
            else:
                for way in (1, -1):
                    offer(what[1], way, "a" if what[0] == "fetch" else "b", 0, r)
            if left[r] == 0 and r < ROUNDS:
                work.append(("complete", r))
                work.extend(("project", r, part, True) for part in range(3))
                if halo:
                    work.extend(halo_work(r))
                else:
                    waiting.append(r)
            continue
        sent = False
        for link, queue in ready.items():
            if queue and busy.get(link, 0.0) - now < backlog:
                queue.sort()
                item = queue.pop(0)[-1]
                actions.append(("send", *item))
                now += 0.05
                sent = True
                if item[0] == "swap":
                    transmit(link, now, cost(item[1], item[2]), item)
                    swaps -= 1
                    if swaps == 0:
                        actions.append(("next",))
                else:
                    kind, axis, way, half, k, r = item
                    transmit(link, now, cost(axis, r), (kind, axis, way, half, k + 1, r))
        if sent:
            continue
        if work:
            item = work.pop(0)
            actions.append(item)
            now += {"project": 0.75, "attend": 2.0}.get(item[0], 0.2)
            continue
        later = [arrivals[0][0]] if arrivals else []
        later += [busy[link] - backlog + 0.01 for link, queue in ready.items() if queue]
        if not later:
            return actions
        now = max(now, min(later))


def kernel(
    x_hbm, w_hbm, wo_hbm, mw_hbm, levels, reach, qgain, kgain,
    vel_hbm, next_hbm,
    weights, out_weights, hidden, own_x, half_x, next_x, mod_weights, part_mod, mod, shift, scale,
    gate, next_gate, queries, keys, values, mixed, next_mixed, vel, stepped,
    send_sem, recv_sem, local_sem,
):
    f = lax.axis_index("frame")
    m = lax.axis_index("mp")
    xl = f % 2
    z = (f // 2) % NZ
    y = f // (2 * NZ)
    xh = m // 2
    c = m % 2

    def frame_of(yy, zz, ll):
        return (yy * NZ + zz) * 2 + ll

    twin = (f, xh * 2 + 1 - c)
    inner = (frame_of(y, z, 1 - xl), m)
    cross = [(frame_of(y, z, 1 - xl), (1 - xh) * 2 + core) for core in range(2)]
    ring = {
        ("z", 1): (frame_of(y, (z + 1) % NZ, xl), m),
        ("z", -1): (frame_of(y, (z + NZ - 1) % NZ, xl), m),
        ("y", 1): (frame_of((y + 1) % NY, z, xl), m),
        ("y", -1): (frame_of((y + NY - 1) % NY, z, xl), m),
    }
    group = [(f, (m + i) % 4) for i in range(1, 4)]
    count = 64
    before = [((f + count - 1) % count, xh * 2 + core) for core in range(2)]
    after = [((f + 1) % count, xh * 2 + core) for core in range(2)]
    chip_before = (f + count - 1 + xh) % count
    chip_after = (f + xh) % count
    halo = [(chip, (1 - xh) * 2 + core) for chip in (chip_before, chip_after) for core in range(2)]

    started = []
    numbers = {}

    def number(key):
        return numbers.setdefault(key, len(numbers))

    def remote(src, dst, key, device, keep=True):
        copy = pltpu.make_async_remote_copy(
            src_ref=src, dst_ref=dst, send_sem=send_sem.at[len(started) if keep else 0],
            recv_sem=recv_sem.at[key if not isinstance(key, tuple) else number(key)],
            device_id=device, device_id_type=MESH,
        )
        return copy

    def send(src, dst, key, device):
        copy = remote(src, dst, key, device)
        started.append(copy)
        copy.start()

    def received(dst, key):
        remote(dst, dst, key, twin, keep=False).wait_recv()

    locals_started = {}

    def load(src, dst, key, place):
        copy = pltpu.make_async_copy(src, dst, local_sem.at[place])
        copy.start()
        locals_started.setdefault(key, []).append(copy)

    barrier = pltpu.get_barrier_semaphore()
    greeted = [twin, inner, *cross, *ring.values(), *group, *before, *after, *halo]
    for device in greeted:
        pl.semaphore_signal(barrier, inc=1, device_id=device, device_id_type=MESH)

    half_columns = pl.multiple_of(c * INNER, INNER)
    other_columns = pl.multiple_of((1 - c) * INNER, INNER)
    own_rows = pl.multiple_of(c * ROWS, ROWS)
    buffers = [weights.at[r] for r in range(ROUNDS)] + [out_weights.at[r] for r in range(2)]
    load(mw_hbm, mod_weights, "mod", 0)
    load(x_hbm, own_x, "x", 1)
    load(x_hbm.at[:, pl.ds(half_columns, INNER)], half_x.at[pl.ds(own_rows, ROWS)], "half", 2)

    def slabs(r, core):
        if r < ROUNDS:
            for part in range(3):
                start = part * INNER + core * HALF + r * PAIR
                yield pl.ds(pl.multiple_of(start, PAIR), PAIR), pl.ds(part * PAIR, PAIR)
        else:
            start = core * INNER + (r - ROUNDS) * WIDE
            yield pl.ds(pl.multiple_of(start, WIDE), WIDE), pl.ds(0, WIDE)

    def source(r):
        return w_hbm if r < ROUNDS else wo_hbm

    def shard_rows(r, owner):
        return pl.ds(pl.multiple_of(owner * SHARD[r], SHARD[r]), SHARD[r])

    for r in range(5):
        for i, (here, there) in enumerate(slabs(r, c)):
            load(source(r).at[:, here], buffers[r].at[shard_rows(r, m), there], r, 3 + 3 * r + i)

    level = jnp.full((16, HEAD), levels[0], jnp.int32).astype(F32)
    sigma_now = flow_sigma((level + 1.0) / NOISE_LEVELS)
    step_size = sigma_now - flow_sigma(level / NOISE_LEVELS)
    index_row = lax.broadcasted_iota(jnp.int32, (16, HEAD), 1).astype(F32)
    angles = 1000.0 * sigma_now * jnp.exp(-math.log(10000.0) * index_row / HEAD)
    waves = [jax.nn.silu(wave(angles)).astype(BF16) for wave in (jnp.cos, jnp.sin)]
    for copy in locals_started.pop("mod"):
        copy.wait()
    columns_mod = jnp.dot(waves[0], mod_weights[:HEAD], preferred_element_type=F32)
    columns_mod += jnp.dot(waves[1], mod_weights[HEAD:], preferred_element_type=F32)
    part_mod[...] = columns_mod[:1]
    mod[m] = columns_mod[:1]
    pl.semaphore_wait(barrier, len(greeted))

    own = {"z": z, "y": y}
    length = {"z": NZ, "y": NY}
    missing = (1 - xh) * 2
    shard_of = {"a": missing + xl, "b": missing + 1 - xl}

    def piece(axis, owner, j, r):
        rows = PIECE[axis][r]
        start = owner * SHARD[r] + BASE[axis][r] + j * rows
        return buffers[r].at[pl.ds(pl.multiple_of(start, 16), rows)]

    fetched = []

    def fetch(r):
        first = len(started)

        @pl.when(c == 1 - xl)
        def _():
            for axis in AXES[r]:
                rows = PIECE[axis][r]
                start = BASE[axis][r] + own[axis] * rows
                rows_here = pl.ds(pl.multiple_of(start, 16), rows)
                rows_there = pl.ds(pl.multiple_of(m * SHARD[r] + start, 16), rows)
                for core in range(2):
                    for here, there in slabs(r, core):
                        send(
                            source(r).at[rows_here, here], buffers[r].at[rows_there, there],
                            ("fetch", axis, r), cross[core],
                        )

        each = (len(started) - first) // len(AXES[r])
        for i in range(first, len(started)):
            rows = PIECE[AXES[r][(i - first) // each]][r]
            region = buffers[r].at[pl.ds(0, rows), pl.ds(0, PAIR if r < ROUNDS else WIDE)]
            started[i] = None
            fetched.append((region, i))

    def exchange(r):
        for here, there in slabs(r, 1 - c):
            send(
                source(r).at[:, here], buffers[r].at[shard_rows(r, m), there], ("twin", r), twin
            )

    def ring_send(axis, way, half, k, r):
        if k >= HOPS[axis, half, way]:
            return
        j = (own[axis] - way * k + length[axis]) % length[axis]
        region = piece(axis, shard_of[half], j, r)
        send(region, region, (axis, way, half, k + 1, r), ring[axis, way])

    def arrived(axis, way, half, k, r):
        j = (own[axis] - way * k + length[axis]) % length[axis]
        received(piece(axis, shard_of[half], j, r), (axis, way, half, k, r))

    def complete(r):
        for copy in locals_started.pop(r):
            copy.wait()
        received(buffers[r].at[shard_rows(r, xh * 2 + 1 - c)], ("twin", r))

    for device in group:
        send(part_mod, mod.at[m], mod_sem_key + m, device)
    fetch(0)
    fetch(1)
    send(
        x_hbm.at[:, pl.ds(other_columns, INNER)], half_x.at[pl.ds(own_rows, ROWS)], ("x",), twin
    )
    for r in range(5):
        exchange(r)
    for r in range(2, 5):
        fetch(r)
    for i in range(1, 4):
        owner = (m + i) % 4
        received(mod.at[owner], mod_sem_key + owner)
    shift[:, :2304] = mod[0]
    shift[:, 2304:] = mod[1, :, :768]
    scale[:, :1536] = 1.0 + mod[1, :, 768:]
    scale[:, 1536:] = 1.0 + mod[2, :, :1536]
    gate[:, :768] = mod[2, :, 1536:]
    gate[:, 768:D] = mod[3]
    gate[:, D:] = step_size[:1]
    slot_before = (f + count - 1) % count
    send(gate, next_gate, ("gate",), (slot_before, m))
    for copy in locals_started.pop("x"):
        copy.wait()

    @pl.loop(0, ROWS // 16)
    def _(i):
        rows = own_x[pl.ds(pl.multiple_of(i * 16, 16), 16), :].astype(F32)
        center = jnp.mean(rows, axis=-1, keepdims=True)
        rows = rows - center
        spread = jnp.mean(rows * rows, axis=-1, keepdims=True)
        out = rows * lax.rsqrt(spread + 1e-06) * scale[...] + shift[...]
        hidden[pl.ds(pl.multiple_of(own_rows + i * 16, 16), 16), :] = out.astype(BF16)

    mine = hidden.at[pl.ds(own_rows, ROWS)]
    send(mine, mine, ("hidden",), twin)
    halo_chip = jnp.where(c == 1, chip_after, chip_before)
    halo_base = jnp.where(c == 1, CHIP, CHIP + ROWS)
    for core in range(2):
        send(
            hidden.at[pl.ds(pl.multiple_of(own_rows + core * SPATIAL, 16), SPATIAL)],
            hidden.at[pl.ds(pl.multiple_of(halo_base + core * SPATIAL, 16), SPATIAL)],
            halo_key + 1 - c, (halo_chip, (1 - xh) * 2 + core),
        )

    def halo_forward():
        for side in range(2):
            region = hidden.at[
                pl.ds(pl.multiple_of(CHIP + side * ROWS + c * SPATIAL, 16), SPATIAL)
            ]
            received(region, halo_key + side)
            send(region, region, ("forward", side), twin)

    def halo_arrived():
        for side in range(2):
            region = hidden.at[
                pl.ds(pl.multiple_of(CHIP + side * ROWS + (1 - c) * SPATIAL, 16), SPATIAL)
            ]
            received(region, ("forward", side))

    def product(lo, r, part):
        return jnp.dot(
            hidden[lo : lo + CHIP, :], weights[r, :, part * PAIR : (part + 1) * PAIR],
            preferred_element_type=F32,
        )

    def normed(tile, gain):
        return tile * lax.rsqrt(jnp.mean(tile * tile, axis=-1, keepdims=True) + 1e-06) * gain

    def project(r, part, own_part):
        tile = product(0 if own_part else CHIP, r, part)
        for h in range(2):
            columns = slice(h * HEAD, (h + 1) * HEAD)
            head = tile[:, columns]
            if part == 0:
                head = normed(head, qgain[...] * (1.0 / math.sqrt(HEAD)))
            elif part == 1:
                head = normed(head, kgain[...])
            head = head.astype(BF16)
            if part == 0:
                queries[r, :, columns] = head
            else:
                target = keys if part == 1 else values
                if own_part:
                    target[r, ROWS : ROWS + CHIP, columns] = head
                else:
                    target[r, 0:ROWS, columns] = head[:ROWS]
                    target[r, ROWS + CHIP :, columns] = head[ROWS:]

    lane = lax.broadcasted_iota(jnp.int32, (1, WINDOW), 1)
    offset = sum((lane >= k * SPATIAL).astype(jnp.int32) for k in range(1, 5)) - REACH_LIMIT

    def attend(r):
        @pl.loop(0, 4)
        def _(i):
            q_rows = pl.ds(pl.multiple_of(i * SPATIAL, 16), SPATIAL)
            k_rows = pl.ds(pl.multiple_of(i * SPATIAL, 16), WINDOW)
            key_frame = f * 8 + xh * 4 + i + offset
            valid = (jnp.abs(offset) <= reach[0]) & (key_frame >= 0) & (key_frame < FRAMES)
            bias = jnp.where(valid, 0.0, -1e30)
            for h in range(2):
                columns = slice(h * HEAD, (h + 1) * HEAD)
                scores = lax.dot_general(
                    queries[r, q_rows, columns], keys[r, k_rows, columns],
                    (((1,), (1,)), ((), ())), preferred_element_type=F32,
                ) + bias
                peak = jnp.max(scores, axis=-1, keepdims=True)
                raised = jnp.exp(scores - peak)
                total = jnp.sum(raised, axis=-1, keepdims=True)
                out = jnp.dot(
                    raised.astype(BF16), values[r, k_rows, columns], preferred_element_type=F32
                )
                place = pl.multiple_of(c * HALF + r * PAIR + h * HEAD, HEAD)
                mixed[q_rows, pl.ds(place, HEAD)] = (out / total).astype(BF16)

        columns = pl.ds(pl.multiple_of(c * HALF + r * PAIR, PAIR), PAIR)
        send(mixed.at[:, columns], next_mixed.at[:, columns], ("next mixed", r), (slot_before, m))
        send(mixed.at[:, columns], mixed.at[:, columns], ("mixed", r), twin)

    def forward_mixed(r):
        region = next_mixed.at[:, pl.ds(pl.multiple_of(c * HALF + r * PAIR, PAIR), PAIR)]
        received(region, ("next mixed", r))
        send(region, region, ("forward mixed", r), twin)

    def all_mixed(buffer, name):
        for r in range(ROUNDS):
            columns = pl.ds(pl.multiple_of((1 - c) * HALF + r * PAIR, PAIR), PAIR)
            received(buffer.at[:, columns], (name, r))

    first = True
    for action in plan():
        kind, rest = action[0], action[1:]
        if kind == "wait":
            kind, rest = rest[0], rest[1:]
            if kind == "fetch":
                received(piece(rest[0], shard_of["a"], own[rest[0]], rest[1]), ("fetch", *rest))
            elif kind == "swap":
                received(piece(rest[0], shard_of["b"], own[rest[0]], rest[1]), ("swap", *rest))
            elif kind == "ring":
                arrived(*rest)
            else:
                halo_forward()
        elif kind == "send":
            kind, rest = rest[0], rest[1:]
            if kind == "swap":
                region = piece(rest[0], shard_of["a"], own[rest[0]], rest[1])
                send(region, region, ("swap", *rest), inner)
            else:
                ring_send(*rest)
        elif kind == "next":
            for core in range(2):
                send(
                    x_hbm.at[:, pl.ds(core * INNER, INNER)], next_x.at[pl.ds(own_rows, ROWS)],
                    next_x_key + c, before[core],
                )
        elif kind == "complete":
            complete(*rest)
            if first:
                other = hidden.at[pl.ds(pl.multiple_of((1 - c) * ROWS, ROWS), ROWS)]
                received(other, ("hidden",))
                first = False
        elif kind == "project":
            project(*rest)
        elif kind == "attend":
            attend(*rest)
        else:
            halo_arrived()

    finals = []

    def finish(buffer, base_rows, gates, out, out_hbm, next_slot):
        for h in range(2):
            for t in range(3):
                lo = h * WIDE + t * PAIR
                attended = jnp.dot(
                    buffer[...], out_weights[h, :, t * PAIR : (t + 1) * PAIR],
                    preferred_element_type=F32,
                )
                gate_row = gates[:, pl.ds(pl.multiple_of(half_columns + lo, PAIR), PAIR)]
                rows = base_rows[:, lo : lo + PAIR].astype(F32)
                full = rows + gate_row * attended
                if next_slot:
                    step = jnp.concatenate([gates[:, D:]] * 2, axis=1)
                    full = rows - step * full
                out[:, lo : lo + PAIR] = full.astype(BF16)
            columns = pl.ds(pl.multiple_of(half_columns + h * WIDE, WIDE), WIDE)
            stage = pl.ds(h * WIDE, WIDE)
            twin_rows = pl.ds(pl.multiple_of((1 - c) * ROWS, ROWS), ROWS)
            send(
                out.at[twin_rows, stage], out_hbm.at[:, columns], ("out", next_slot, h), twin
            )
            copy = pltpu.make_async_copy(
                out.at[pl.ds(own_rows, ROWS), stage], out_hbm.at[:, columns],
                local_sem.at[18 + len(finals)],
            )
            copy.start()
            finals.append(copy)

    forward_mixed(0)
    complete(3)
    complete(4)
    for copy in locals_started.pop("half"):
        copy.wait()
    received(half_x.at[pl.ds(pl.multiple_of((1 - c) * ROWS, ROWS), ROWS)], ("x",))
    all_mixed(mixed, "mixed")
    finish(mixed, half_x, gate, vel, vel_hbm, False)
    forward_mixed(1)
    forward_mixed(2)
    received(next_gate, ("gate",))
    for core in range(2):
        received(next_x.at[pl.ds(core * ROWS, ROWS)], next_x_key + core)
    all_mixed(next_mixed, "forward mixed")
    finish(next_mixed, next_x, next_gate, stepped, next_hbm, True)
    for h in range(2):
        columns = pl.ds(pl.multiple_of(other_columns + h * WIDE, WIDE), WIDE)
        received(vel_hbm.at[:, columns], ("out", False, h))
        received(next_hbm.at[:, columns], ("out", True, h))
    for copy in finals:
        copy.wait()
    assert len(started) <= SENDS and len(numbers) <= mod_sem_key
    for copy in started:
        if copy is not None:
            copy.wait_send()

    @pl.when(c == 1 - xl)
    def _():
        for region, i in fetched:
            pltpu.make_async_remote_copy(
                src_ref=region, dst_ref=region, send_sem=send_sem.at[i], recv_sem=recv_sem.at[0],
                device_id=twin, device_id_type=MESH,
            ).wait_send()


mod_sem_key = 160
halo_key = 164
next_x_key = 166
SEMAPHORES = 168
SENDS = 288


def per_device(
    latents, levels, window_reach, query_gain, key_gain, qkv_weight, out_weight, mod_weight
):
    vmem = pl.BlockSpec(memory_space=pltpu.VMEM)
    smem = pl.BlockSpec(memory_space=pltpu.SMEM)
    hbm = pl.BlockSpec(memory_space=pl.ANY)
    shape = jax.ShapeDtypeStruct((ROWS, D), BF16)
    velocity, queue_next = pl.pallas_call(
        kernel,
        out_shape=(shape, shape),
        in_specs=[hbm, hbm, hbm, hbm, smem, smem, vmem, vmem],
        out_specs=(hbm, hbm),
        scratch_shapes=[
            pltpu.VMEM((ROUNDS, D, WIDE), BF16),
            pltpu.VMEM((2, INNER, WIDE), BF16),
            pltpu.VMEM((2 * CHIP, D), BF16),
            pltpu.VMEM((ROWS, D), BF16),
            pltpu.VMEM((CHIP, INNER), BF16),
            pltpu.VMEM((CHIP, INNER), BF16),
            pltpu.VMEM((FREQ, 2304), BF16),
            pltpu.VMEM((1, 2304), F32),
            pltpu.VMEM((4, 1, 2304), F32),
            pltpu.VMEM((1, D), F32),
            pltpu.VMEM((1, D), F32),
            pltpu.VMEM((1, D + HEAD), F32),
            pltpu.VMEM((1, D + HEAD), F32),
            pltpu.VMEM((ROUNDS, CHIP, PAIR), BF16),
            pltpu.VMEM((ROUNDS, 2 * CHIP, PAIR), BF16),
            pltpu.VMEM((ROUNDS, 2 * CHIP, PAIR), BF16),
            pltpu.VMEM((CHIP, INNER), BF16),
            pltpu.VMEM((CHIP, INNER), BF16),
            pltpu.VMEM((CHIP, INNER), BF16),
            pltpu.VMEM((CHIP, INNER), BF16),
            pltpu.SemaphoreType.DMA((SENDS,)),
            pltpu.SemaphoreType.DMA((SEMAPHORES,)),
            pltpu.SemaphoreType.DMA((24,)),
        ],
        compiler_params=pltpu.CompilerParams(
            collective_id=0, has_side_effects=True, vmem_limit_bytes=56 * 2**20
        ),
    )(
        latents.reshape(ROWS, D), qkv_weight, out_weight, mod_weight, levels, window_reach,
        query_gain.reshape(1, HEAD), key_gain.reshape(1, HEAD),
    )
    return (queue_next.reshape(2, SPATIAL, D), velocity.reshape(2, SPATIAL, D))


def solution(mesh):
    return jax.shard_map(
        per_device,
        mesh=mesh,
        in_specs=(
            P(("frame", "mp"), None, None),
            P("frame"),
            P("frame"),
            P(),
            P(),
            P("mp", None),
            P("mp", None),
            P(None, "mp"),
        ),
        out_specs=(P(("frame", "mp"), None, None), P(("frame", "mp"), None, None)),
        check_vma=False,
    )
```

```python
import heapq
import math

import jax
import jax.numpy as jnp
from jax import lax
from jax.experimental import pallas as pl
from jax.experimental.pallas import tpu as pltpu
from jax.sharding import PartitionSpec as P

D = 3072
HEADS = 12
HEAD = 128
FREQ = 256
NOISE_LEVELS = 50
REACH_LIMIT = 2
SPATIAL = 96
FRAMES = 512
INNER = HEADS * HEAD
ROWS = 2 * SPATIAL
CHIP = 2 * ROWS
HALF = INNER // 2
PAIR = 2 * HEAD
WINDOW = (2 * REACH_LIMIT + 1) * SPATIAL
ROUNDS = 3
NY, NZ = 4, 8
MESH = pl.DeviceIdType.MESH
F32 = jnp.float32
BF16 = jnp.bfloat16

flow_shift = 7.0


def flow_sigma(position):
    return flow_shift * position / (1.0 + (flow_shift - 1.0) * position)


HOPS = {
    ("z", "a", 1): 4, ("z", "a", -1): 3, ("z", "b", 1): 3, ("z", "b", -1): 4,
    ("y", "a", 1): 2, ("y", "a", -1): 1, ("y", "b", 1): 1, ("y", "b", -1): 2,
}
SHARD = [768] * ROUNDS + [384] * 2
PIECE = {"z": [48] * ROUNDS + [0] * 2, "y": [96] * ROUNDS + [96] * 2}
BASE = {"z": [0] * 5, "y": [384] * ROUNDS + [0] * 2}
AXES = [[axis for axis in "zy" if PIECE[axis][r]] for r in range(5)]
WIDE = 3 * PAIR
HALO_TIMES = [6.0, 6.01]
NEXT_TIMES = [6.1, 6.11, 6.12, 6.13]


def plan():
    rate, latency, backlog, halo_time = 46500.0, 4.0, 100.0, 25.0
    busy, ready, arrivals, actions, work, waiting = {}, {}, [], [], [], []

    def cost(axis, r):
        return PIECE[axis][r] * WIDE * 2 / rate

    def transmit(link, time, length, what):
        busy[link] = max(busy.get(link, 0.0), time) + length
        heapq.heappush(arrivals, (busy[link] + latency, len(actions), len(arrivals), what))

    def offer(axis, way, half, k, r):
        rest = HOPS[axis, half, way] - k
        if rest > 0:
            item = (r, -rest, len(actions), ("ring", axis, way, half, k, r))
            ready.setdefault((axis, way), []).append(item)

    left = [0] * 5
    for r in range(5):
        for axis in AXES[r]:
            left[r] += 2 + sum(hops for key, hops in HOPS.items() if key[0] == axis)
            transmit("cross", 0.0, cost(axis, r), ("fetch", axis, r))
    now = 6.0
    for time in HALO_TIMES + NEXT_TIMES:
        what = ("halo send",) if time in HALO_TIMES else ("next send",)
        heapq.heappush(arrivals, (time, 0, len(arrivals), what))
    halo = False
    halos = 0

    def halo_work(r):
        return [("project", r, 1, False), ("project", r, 2, False), ("attend", r)]

    while True:
        if arrivals and arrivals[0][0] <= now:
            what = heapq.heappop(arrivals)[-1]
            now += 0.05
            if what[0] == "halo send":
                actions.append(("halo send", halos))
                halos += 1
                if halos == len(HALO_TIMES):
                    transmit("cross", now, halo_time, ("halo",))
                continue
            if what[0] == "next send":
                actions.append(("next", len([0 for action in actions if action[0] == "next"])))
                continue
            actions.append(("wait", *what))
            if what[0] == "halo":
                halo = True
                work.append(("halo",))
                for r in waiting:
                    work.extend(halo_work(r))
                continue
            r = what[-1]
            left[r] -= 1
            if what[0] == "fetch":
                ready.setdefault("inner", []).append((r, 0, len(actions), ("swap", what[1], r)))
            if what[0] == "ring":
                offer(*what[1:])
            else:
                for way in (1, -1):
                    offer(what[1], way, "a" if what[0] == "fetch" else "b", 0, r)
            if left[r] == 0 and r < ROUNDS:
                work.append(("complete", r))
                work.extend(("project", r, part, True) for part in range(3))
                if halo:
                    work.extend(halo_work(r))
                else:
                    waiting.append(r)
            continue
        sent = False
        for link, queue in ready.items():
            if queue and busy.get(link, 0.0) - now < backlog:
                queue.sort()
                item = queue.pop(0)[-1]
                actions.append(("send", *item))
                now += 0.05
                sent = True
                if item[0] == "swap":
                    transmit(link, now, cost(item[1], item[2]), item)
                else:
                    kind, axis, way, half, k, r = item
                    transmit(link, now, cost(axis, r), (kind, axis, way, half, k + 1, r))
        if sent:
            continue
        if work:
            item = work.pop(0)
            actions.append(item)
            now += {"project": 0.75, "attend": 2.0}.get(item[0], 0.2)
            continue
        later = [arrivals[0][0]] if arrivals else []
        later += [busy[link] - backlog + 0.01 for link, queue in ready.items() if queue]
        if not later:
            return actions
        now = max(now, min(later))


def kernel(
    x_hbm, w_hbm, wo_hbm, mw_hbm, levels, reach, qgain, kgain,
    vel_hbm, next_hbm,
    weights, out_weights, hidden, own_x, half_x, next_x, mod_weights, part_mod, mod, shift, scale,
    gate, next_gate, queries, keys, values, mixed, next_mixed, vel, stepped,
    send_sem, recv_sem, local_sem,
):
    f = lax.axis_index("frame")
    m = lax.axis_index("mp")
    xl = f % 2
    z = (f // 2) % NZ
    y = f // (2 * NZ)
    xh = m // 2
    c = m % 2

    def frame_of(yy, zz, ll):
        return (yy * NZ + zz) * 2 + ll

    twin = (f, xh * 2 + 1 - c)
    inner = (frame_of(y, z, 1 - xl), m)
    cross = [(frame_of(y, z, 1 - xl), (1 - xh) * 2 + core) for core in range(2)]
    ring = {
        ("z", 1): (frame_of(y, (z + 1) % NZ, xl), m),
        ("z", -1): (frame_of(y, (z + NZ - 1) % NZ, xl), m),
        ("y", 1): (frame_of((y + 1) % NY, z, xl), m),
        ("y", -1): (frame_of((y + NY - 1) % NY, z, xl), m),
    }
    group = [(f, (m + i) % 4) for i in range(1, 4)]
    count = 64
    before = [((f + count - 1) % count, xh * 2 + core) for core in range(2)]
    after = [((f + 1) % count, xh * 2 + core) for core in range(2)]
    chip_before = (f + count - 1 + xh) % count
    chip_after = (f + xh) % count
    halo = [(chip, (1 - xh) * 2 + core) for chip in (chip_before, chip_after) for core in range(2)]

    started = []
    numbers = {}

    def number(key):
        return numbers.setdefault(key, len(numbers))

    def remote(src, dst, key, device, keep=True):
        copy = pltpu.make_async_remote_copy(
            src_ref=src, dst_ref=dst, send_sem=send_sem.at[len(started) if keep else 0],
            recv_sem=recv_sem.at[key if not isinstance(key, tuple) else number(key)],
            device_id=device, device_id_type=MESH,
        )
        return copy

    def send(src, dst, key, device):
        copy = remote(src, dst, key, device)
        started.append(copy)
        copy.start()

    def received(dst, key):
        remote(dst, dst, key, twin, keep=False).wait_recv()

    locals_started = {}

    def load(src, dst, key, place):
        copy = pltpu.make_async_copy(src, dst, local_sem.at[place])
        copy.start()
        locals_started.setdefault(key, []).append(copy)

    barrier = pltpu.get_barrier_semaphore()
    greeted = [twin, inner, *cross, *ring.values(), *group, *before, *after, *halo]
    for device in greeted:
        pl.semaphore_signal(barrier, inc=1, device_id=device, device_id_type=MESH)

    half_columns = pl.multiple_of(c * INNER, INNER)
    other_columns = pl.multiple_of((1 - c) * INNER, INNER)
    own_rows = pl.multiple_of(c * ROWS, ROWS)
    buffers = [weights.at[r] for r in range(ROUNDS)] + [out_weights.at[r] for r in range(2)]
    load(mw_hbm, mod_weights, "mod", 0)
    load(x_hbm, own_x, "x", 1)
    load(x_hbm.at[:, pl.ds(half_columns, INNER)], half_x.at[pl.ds(own_rows, ROWS)], "half", 2)

    def slabs(r, core):
        if r < ROUNDS:
            for part in range(3):
                start = part * INNER + core * HALF + r * PAIR
                yield pl.ds(pl.multiple_of(start, PAIR), PAIR), pl.ds(part * PAIR, PAIR)
        else:
            start = core * INNER + (r - ROUNDS) * WIDE
            yield pl.ds(pl.multiple_of(start, WIDE), WIDE), pl.ds(0, WIDE)

    def source(r):
        return w_hbm if r < ROUNDS else wo_hbm

    def shard_rows(r, owner):
        return pl.ds(pl.multiple_of(owner * SHARD[r], SHARD[r]), SHARD[r])

    for r in range(5):
        for i, (here, there) in enumerate(slabs(r, c)):
            load(source(r).at[:, here], buffers[r].at[shard_rows(r, m), there], r, 3 + 3 * r + i)

    level = jnp.full((16, HEAD), levels[0], jnp.int32).astype(F32)
    sigma_now = flow_sigma((level + 1.0) / NOISE_LEVELS)
    step_size = sigma_now - flow_sigma(level / NOISE_LEVELS)
    index_row = lax.broadcasted_iota(jnp.int32, (16, HEAD), 1).astype(F32)
    angles = 1000.0 * sigma_now * jnp.exp(-math.log(10000.0) * index_row / HEAD)
    waves = [jax.nn.silu(wave(angles)).astype(BF16) for wave in (jnp.cos, jnp.sin)]
    for copy in locals_started.pop("mod"):
        copy.wait()
    columns_mod = jnp.dot(waves[0], mod_weights[:HEAD], preferred_element_type=F32)
    columns_mod += jnp.dot(waves[1], mod_weights[HEAD:], preferred_element_type=F32)
    part_mod[...] = columns_mod[:1]
    mod[m] = columns_mod[:1]
    pl.semaphore_wait(barrier, len(greeted))

    own = {"z": z, "y": y}
    length = {"z": NZ, "y": NY}
    missing = (1 - xh) * 2
    shard_of = {"a": missing + xl, "b": missing + 1 - xl}

    def piece(axis, owner, j, r):
        rows = PIECE[axis][r]
        start = owner * SHARD[r] + BASE[axis][r] + j * rows
        return buffers[r].at[pl.ds(pl.multiple_of(start, 16), rows)]

    fetched = []

    def fetch(r):
        first = len(started)

        @pl.when(c == 1 - xl)
        def _():
            for axis in AXES[r]:
                rows = PIECE[axis][r]
                start = BASE[axis][r] + own[axis] * rows
                rows_here = pl.ds(pl.multiple_of(start, 16), rows)
                rows_there = pl.ds(pl.multiple_of(m * SHARD[r] + start, 16), rows)
                for core in range(2):
                    for here, there in slabs(r, core):
                        send(
                            source(r).at[rows_here, here], buffers[r].at[rows_there, there],
                            ("fetch", axis, r), cross[core],
                        )

        each = (len(started) - first) // len(AXES[r])
        for i in range(first, len(started)):
            rows = PIECE[AXES[r][(i - first) // each]][r]
            region = buffers[r].at[pl.ds(0, rows), pl.ds(0, PAIR if r < ROUNDS else WIDE)]
            started[i] = None
            fetched.append((region, i))

    def exchange(r):
        for here, there in slabs(r, 1 - c):
            send(
                source(r).at[:, here], buffers[r].at[shard_rows(r, m), there], ("twin", r), twin
            )

    def ring_send(axis, way, half, k, r):
        if k >= HOPS[axis, half, way]:
            return
        j = (own[axis] - way * k + length[axis]) % length[axis]
        region = piece(axis, shard_of[half], j, r)
        send(region, region, (axis, way, half, k + 1, r), ring[axis, way])

    def arrived(axis, way, half, k, r):
        j = (own[axis] - way * k + length[axis]) % length[axis]
        received(piece(axis, shard_of[half], j, r), (axis, way, half, k, r))

    def complete(r):
        for copy in locals_started.pop(r):
            copy.wait()
        received(buffers[r].at[shard_rows(r, xh * 2 + 1 - c)], ("twin", r))

    for device in group:
        send(part_mod, mod.at[m], mod_sem_key + m, device)
    fetch(0)
    fetch(1)
    send(
        x_hbm.at[:, pl.ds(other_columns, INNER)], half_x.at[pl.ds(own_rows, ROWS)], ("x",), twin
    )
    for r in range(5):
        exchange(r)
    for r in range(2, 5):
        fetch(r)
    for i in range(1, 4):
        owner = (m + i) % 4
        received(mod.at[owner], mod_sem_key + owner)
    shift[:, :2304] = mod[0]
    shift[:, 2304:] = mod[1, :, :768]
    scale[:, :1536] = 1.0 + mod[1, :, 768:]
    scale[:, 1536:] = 1.0 + mod[2, :, :1536]
    gate[:, :768] = mod[2, :, 1536:]
    gate[:, 768:D] = mod[3]
    gate[:, D:] = step_size[:1]
    slot_before = (f + count - 1) % count
    send(gate, next_gate, ("gate",), (slot_before, m))
    for copy in locals_started.pop("x"):
        copy.wait()

    @pl.loop(0, ROWS // 16)
    def _(i):
        rows = own_x[pl.ds(pl.multiple_of(i * 16, 16), 16), :].astype(F32)
        center = jnp.mean(rows, axis=-1, keepdims=True)
        rows = rows - center
        spread = jnp.mean(rows * rows, axis=-1, keepdims=True)
        out = rows * lax.rsqrt(spread + 1e-06) * scale[...] + shift[...]
        hidden[pl.ds(pl.multiple_of(own_rows + i * 16, 16), 16), :] = out.astype(BF16)

    mine = hidden.at[pl.ds(own_rows, ROWS)]
    send(mine, mine, ("hidden",), twin)
    halo_chip = jnp.where(c == 1, chip_after, chip_before)
    halo_base = jnp.where(c == 1, CHIP, CHIP + ROWS)

    def halo_send(core):
        send(
            hidden.at[pl.ds(pl.multiple_of(own_rows + core * SPATIAL, 16), SPATIAL)],
            hidden.at[pl.ds(pl.multiple_of(halo_base + core * SPATIAL, 16), SPATIAL)],
            halo_key + 1 - c, (halo_chip, (1 - xh) * 2 + core),
        )

    def next_send(i):
        core, part = i % 2, i // 2
        rows = ROWS * 2 // len(NEXT_TIMES)
        send(
            x_hbm.at[pl.ds(part * rows, rows), pl.ds(core * INNER, INNER)],
            next_x.at[pl.ds(pl.multiple_of(own_rows + part * rows, 16), rows)],
            next_x_key + c, before[core],
        )

    def halo_forward():
        for side in range(2):
            region = hidden.at[
                pl.ds(pl.multiple_of(CHIP + side * ROWS + c * SPATIAL, 16), SPATIAL)
            ]
            received(region, halo_key + side)
            send(region, region, ("forward", side), twin)

    def halo_arrived():
        for side in range(2):
            region = hidden.at[
                pl.ds(pl.multiple_of(CHIP + side * ROWS + (1 - c) * SPATIAL, 16), SPATIAL)
            ]
            received(region, ("forward", side))

    def product(lo, r, part):
        return jnp.dot(
            hidden[lo : lo + CHIP, :], weights[r, :, part * PAIR : (part + 1) * PAIR],
            preferred_element_type=F32,
        )

    def normed(tile, gain):
        return tile * lax.rsqrt(jnp.mean(tile * tile, axis=-1, keepdims=True) + 1e-06) * gain

    def project(r, part, own_part):
        tile = product(0 if own_part else CHIP, r, part)
        for h in range(2):
            columns = slice(h * HEAD, (h + 1) * HEAD)
            head = tile[:, columns]
            if part == 0:
                head = normed(head, qgain[...] * (1.0 / math.sqrt(HEAD)))
            elif part == 1:
                head = normed(head, kgain[...])
            head = head.astype(BF16)
            if part == 0:
                queries[r, :, columns] = head
            else:
                target = keys if part == 1 else values
                if own_part:
                    target[r, ROWS : ROWS + CHIP, columns] = head
                else:
                    target[r, 0:ROWS, columns] = head[:ROWS]
                    target[r, ROWS + CHIP :, columns] = head[ROWS:]

    lane = lax.broadcasted_iota(jnp.int32, (1, WINDOW), 1)
    offset = sum((lane >= k * SPATIAL).astype(jnp.int32) for k in range(1, 5)) - REACH_LIMIT

    def attend(r):
        @pl.loop(0, 4)
        def _(i):
            q_rows = pl.ds(pl.multiple_of(i * SPATIAL, 16), SPATIAL)
            k_rows = pl.ds(pl.multiple_of(i * SPATIAL, 16), WINDOW)
            key_frame = f * 8 + xh * 4 + i + offset
            valid = (jnp.abs(offset) <= reach[0]) & (key_frame >= 0) & (key_frame < FRAMES)
            bias = jnp.where(valid, 0.0, -1e30)
            for h in range(2):
                columns = slice(h * HEAD, (h + 1) * HEAD)
                scores = lax.dot_general(
                    queries[r, q_rows, columns], keys[r, k_rows, columns],
                    (((1,), (1,)), ((), ())), preferred_element_type=F32,
                ) + bias
                peak = jnp.max(scores, axis=-1, keepdims=True)
                raised = jnp.exp(scores - peak)
                total = jnp.sum(raised, axis=-1, keepdims=True)
                out = jnp.dot(
                    raised.astype(BF16), values[r, k_rows, columns], preferred_element_type=F32
                )
                place = pl.multiple_of(c * HALF + r * PAIR + h * HEAD, HEAD)
                mixed[q_rows, pl.ds(place, HEAD)] = (out / total).astype(BF16)

        columns = pl.ds(pl.multiple_of(c * HALF + r * PAIR, PAIR), PAIR)
        send(mixed.at[:, columns], next_mixed.at[:, columns], ("next mixed", r), (slot_before, m))
        send(mixed.at[:, columns], mixed.at[:, columns], ("mixed", r), twin)

    def forward_mixed(r):
        region = next_mixed.at[:, pl.ds(pl.multiple_of(c * HALF + r * PAIR, PAIR), PAIR)]
        received(region, ("next mixed", r))
        send(region, region, ("forward mixed", r), twin)

    def all_mixed(buffer, name):
        for r in range(ROUNDS):
            columns = pl.ds(pl.multiple_of((1 - c) * HALF + r * PAIR, PAIR), PAIR)
            received(buffer.at[:, columns], (name, r))

    first = True
    for action in plan():
        kind, rest = action[0], action[1:]
        if kind == "wait":
            kind, rest = rest[0], rest[1:]
            if kind == "fetch":
                received(piece(rest[0], shard_of["a"], own[rest[0]], rest[1]), ("fetch", *rest))
            elif kind == "swap":
                received(piece(rest[0], shard_of["b"], own[rest[0]], rest[1]), ("swap", *rest))
            elif kind == "ring":
                arrived(*rest)
            else:
                halo_forward()
        elif kind == "send":
            kind, rest = rest[0], rest[1:]
            if kind == "swap":
                region = piece(rest[0], shard_of["a"], own[rest[0]], rest[1])
                send(region, region, ("swap", *rest), inner)
            else:
                ring_send(*rest)
        elif kind == "halo send":
            halo_send(*rest)
        elif kind == "next":
            next_send(*rest)
        elif kind == "complete":
            complete(*rest)
            if first:
                other = hidden.at[pl.ds(pl.multiple_of((1 - c) * ROWS, ROWS), ROWS)]
                received(other, ("hidden",))
                first = False
        elif kind == "project":
            project(*rest)
        elif kind == "attend":
            attend(*rest)
        else:
            halo_arrived()

    finals = []

    def finish(buffer, base_rows, gates, out, out_hbm, next_slot):
        for h in range(2):
            for t in range(3):
                lo = h * WIDE + t * PAIR
                attended = jnp.dot(
                    buffer[...], out_weights[h, :, t * PAIR : (t + 1) * PAIR],
                    preferred_element_type=F32,
                )
                gate_row = gates[:, pl.ds(pl.multiple_of(half_columns + lo, PAIR), PAIR)]
                rows = base_rows[:, lo : lo + PAIR].astype(F32)
                full = rows + gate_row * attended
                if next_slot:
                    step = jnp.concatenate([gates[:, D:]] * 2, axis=1)
                    full = rows - step * full
                out[:, lo : lo + PAIR] = full.astype(BF16)
            columns = pl.ds(pl.multiple_of(half_columns + h * WIDE, WIDE), WIDE)
            stage = pl.ds(h * WIDE, WIDE)
            twin_rows = pl.ds(pl.multiple_of((1 - c) * ROWS, ROWS), ROWS)
            send(
                out.at[twin_rows, stage], out_hbm.at[:, columns], ("out", next_slot, h), twin
            )
            copy = pltpu.make_async_copy(
                out.at[pl.ds(own_rows, ROWS), stage], out_hbm.at[:, columns],
                local_sem.at[18 + len(finals)],
            )
            copy.start()
            finals.append(copy)

    forward_mixed(0)
    complete(3)
    complete(4)
    for copy in locals_started.pop("half"):
        copy.wait()
    received(half_x.at[pl.ds(pl.multiple_of((1 - c) * ROWS, ROWS), ROWS)], ("x",))
    all_mixed(mixed, "mixed")
    finish(mixed, half_x, gate, vel, vel_hbm, False)
    forward_mixed(1)
    forward_mixed(2)
    received(next_gate, ("gate",))
    for core in range(2):
        received(next_x.at[pl.ds(core * ROWS, ROWS)], next_x_key + core)
    all_mixed(next_mixed, "forward mixed")
    finish(next_mixed, next_x, next_gate, stepped, next_hbm, True)
    for h in range(2):
        columns = pl.ds(pl.multiple_of(other_columns + h * WIDE, WIDE), WIDE)
        received(vel_hbm.at[:, columns], ("out", False, h))
        received(next_hbm.at[:, columns], ("out", True, h))
    for copy in finals:
        copy.wait()
    assert len(started) <= SENDS and len(numbers) <= mod_sem_key
    for copy in started:
        if copy is not None:
            copy.wait_send()

    @pl.when(c == 1 - xl)
    def _():
        for region, i in fetched:
            pltpu.make_async_remote_copy(
                src_ref=region, dst_ref=region, send_sem=send_sem.at[i], recv_sem=recv_sem.at[0],
                device_id=twin, device_id_type=MESH,
            ).wait_send()


mod_sem_key = 160
halo_key = 164
next_x_key = 166
SEMAPHORES = 168
SENDS = 288


def per_device(
    latents, levels, window_reach, query_gain, key_gain, qkv_weight, out_weight, mod_weight
):
    vmem = pl.BlockSpec(memory_space=pltpu.VMEM)
    smem = pl.BlockSpec(memory_space=pltpu.SMEM)
    hbm = pl.BlockSpec(memory_space=pl.ANY)
    shape = jax.ShapeDtypeStruct((ROWS, D), BF16)
    velocity, queue_next = pl.pallas_call(
        kernel,
        out_shape=(shape, shape),
        in_specs=[hbm, hbm, hbm, hbm, smem, smem, vmem, vmem],
        out_specs=(hbm, hbm),
        scratch_shapes=[
            pltpu.VMEM((ROUNDS, D, WIDE), BF16),
            pltpu.VMEM((2, INNER, WIDE), BF16),
            pltpu.VMEM((2 * CHIP, D), BF16),
            pltpu.VMEM((ROWS, D), BF16),
            pltpu.VMEM((CHIP, INNER), BF16),
            pltpu.VMEM((CHIP, INNER), BF16),
            pltpu.VMEM((FREQ, 2304), BF16),
            pltpu.VMEM((1, 2304), F32),
            pltpu.VMEM((4, 1, 2304), F32),
            pltpu.VMEM((1, D), F32),
            pltpu.VMEM((1, D), F32),
            pltpu.VMEM((1, D + HEAD), F32),
            pltpu.VMEM((1, D + HEAD), F32),
            pltpu.VMEM((ROUNDS, CHIP, PAIR), BF16),
            pltpu.VMEM((ROUNDS, 2 * CHIP, PAIR), BF16),
            pltpu.VMEM((ROUNDS, 2 * CHIP, PAIR), BF16),
            pltpu.VMEM((CHIP, INNER), BF16),
            pltpu.VMEM((CHIP, INNER), BF16),
            pltpu.VMEM((CHIP, INNER), BF16),
            pltpu.VMEM((CHIP, INNER), BF16),
            pltpu.SemaphoreType.DMA((SENDS,)),
            pltpu.SemaphoreType.DMA((SEMAPHORES,)),
            pltpu.SemaphoreType.DMA((24,)),
        ],
        compiler_params=pltpu.CompilerParams(
            collective_id=0, has_side_effects=True, vmem_limit_bytes=56 * 2**20
        ),
    )(
        latents.reshape(ROWS, D), qkv_weight, out_weight, mod_weight, levels, window_reach,
        query_gain.reshape(1, HEAD), key_gain.reshape(1, HEAD),
    )
    return (queue_next.reshape(2, SPATIAL, D), velocity.reshape(2, SPATIAL, D))


def solution(mesh):
    return jax.shard_map(
        per_device,
        mesh=mesh,
        in_specs=(
            P(("frame", "mp"), None, None),
            P("frame"),
            P("frame"),
            P(),
            P(),
            P("mp", None),
            P("mp", None),
            P(None, "mp"),
        ),
        out_specs=(P(("frame", "mp"), None, None), P(("frame", "mp"), None, None)),
        check_vma=False,
    )
```

```python
import heapq
import math

import jax
import jax.numpy as jnp
from jax import lax
from jax.experimental import pallas as pl
from jax.experimental.pallas import tpu as pltpu
from jax.sharding import PartitionSpec as P

D = 3072
HEADS = 12
HEAD = 128
FREQ = 256
NOISE_LEVELS = 50
REACH_LIMIT = 2
SPATIAL = 96
FRAMES = 512
INNER = HEADS * HEAD
ROWS = 2 * SPATIAL
CHIP = 2 * ROWS
HALF = INNER // 2
PAIR = 2 * HEAD
WINDOW = (2 * REACH_LIMIT + 1) * SPATIAL
ROUNDS = 3
NY, NZ = 4, 8
MESH = pl.DeviceIdType.MESH
F32 = jnp.float32
BF16 = jnp.bfloat16

flow_shift = 7.0


def flow_sigma(position):
    return flow_shift * position / (1.0 + (flow_shift - 1.0) * position)


HOPS = {
    ("z", "a", 1): 4, ("z", "a", -1): 3, ("z", "b", 1): 3, ("z", "b", -1): 4,
    ("y", "a", 1): 2, ("y", "a", -1): 1, ("y", "b", 1): 1, ("y", "b", -1): 2,
}
SHARD = [768] * ROUNDS + [384] * 2
PIECE = {"z": [48] * ROUNDS + [0] * 2, "y": [96] * ROUNDS + [96] * 2}
BASE = {"z": [0] * 5, "y": [384] * ROUNDS + [0] * 2}
AXES = [[axis for axis in "zy" if PIECE[axis][r]] for r in range(5)]
DIRECT = ()
WIDE = 3 * PAIR
RELAY_TIMES = [18.0, 28.0]
HALO_TIME = 36.0


def plan():
    rate, latency, backlog = 46500.0, 4.0, 100.0
    busy, ready, arrivals, actions, work, waiting = {}, {}, [], [], [], []

    def cost(axis, r):
        return PIECE[axis][r] * WIDE * 2 / rate

    def transmit(link, time, length, what):
        busy[link] = max(busy.get(link, 0.0), time) + length
        heapq.heappush(arrivals, (busy[link] + latency, len(actions), len(arrivals), what))

    def offer(axis, way, half, k, r):
        rest = HOPS[axis, half, way] - k
        if rest > 0:
            item = (r, -rest, len(actions), ("ring", axis, way, half, k, r))
            ready.setdefault((axis, way), []).append(item)

    left = [0] * 5
    for r in range(5):
        for axis in AXES[r]:
            left[r] += 2 + sum(hops for key, hops in HOPS.items() if key[0] == axis)
            for what in ("fetch", "swap") if r in DIRECT else ("fetch",):
                transmit("cross", 0.0, cost(axis, r), (what, axis, r))
    now = 6.0
    for i, time in enumerate(RELAY_TIMES):
        heapq.heappush(arrivals, (time, 0, len(arrivals), ("relay", i)))
    heapq.heappush(arrivals, (HALO_TIME, 0, len(arrivals), ("halo",)))
    halo = False

    def halo_work(r):
        return [("project", r, 1, False), ("project", r, 2, False), ("attend", r)]

    while True:
        if arrivals and arrivals[0][0] <= now:
            what = heapq.heappop(arrivals)[-1]
            now += 0.05
            if what[0] == "relay":
                actions.append(what)
                continue
            actions.append(("wait", *what))
            if what[0] == "halo":
                halo = True
                work.append(("halo",))
                for r in waiting:
                    work.extend(halo_work(r))
                continue
            r = what[-1]
            left[r] -= 1
            if what[0] == "fetch" and r not in DIRECT:
                ready.setdefault("inner", []).append((r, 0, len(actions), ("swap", what[1], r)))
            if what[0] == "ring":
                offer(*what[1:])
            else:
                for way in (1, -1):
                    offer(what[1], way, "a" if what[0] == "fetch" else "b", 0, r)
            if left[r] == 0 and r < ROUNDS:
                work.append(("complete", r))
                work.extend(("project", r, part, True) for part in range(3))
                if halo:
                    work.extend(halo_work(r))
                else:
                    waiting.append(r)
            continue
        sent = False
        for link, queue in ready.items():
            if queue and busy.get(link, 0.0) - now < backlog:
                queue.sort()
                item = queue.pop(0)[-1]
                actions.append(("send", *item))
                now += 0.05
                sent = True
                if item[0] == "swap":
                    transmit(link, now, cost(item[1], item[2]), item)
                else:
                    kind, axis, way, half, k, r = item
                    transmit(link, now, cost(axis, r), (kind, axis, way, half, k + 1, r))
        if sent:
            continue
        if work:
            item = work.pop(0)
            actions.append(item)
            now += {"project": 0.75, "attend": 2.0}.get(item[0], 0.2)
            continue
        later = [arrivals[0][0]] if arrivals else []
        later += [busy[link] - backlog + 0.01 for link, queue in ready.items() if queue]
        if not later:
            return actions
        now = max(now, min(later))


def kernel(
    x_hbm, w_hbm, wo_hbm, mw_hbm, levels, reach, qgain, kgain,
    vel_hbm, next_hbm,
    weights, out_weights, hidden, own_x, half_x, next_x, mod_weights, part_mod, mod, shift, scale,
    gate, next_gate, relay_rows, queries, keys, values, mixed, next_mixed, vel, stepped,
    send_sem, recv_sem, local_sem,
):
    f = lax.axis_index("frame")
    m = lax.axis_index("mp")
    xl = f % 2
    z = (f // 2) % NZ
    y = f // (2 * NZ)
    xh = m // 2
    c = m % 2

    def frame_of(yy, zz, ll):
        return (yy * NZ + zz) * 2 + ll

    twin = (f, xh * 2 + 1 - c)
    inner = (frame_of(y, z, 1 - xl), m)
    cross = [(frame_of(y, z, 1 - xl), (1 - xh) * 2 + core) for core in range(2)]
    ring = {
        ("z", 1): (frame_of(y, (z + 1) % NZ, xl), m),
        ("z", -1): (frame_of(y, (z + NZ - 1) % NZ, xl), m),
        ("y", 1): (frame_of((y + 1) % NY, z, xl), m),
        ("y", -1): (frame_of((y + NY - 1) % NY, z, xl), m),
    }
    group = [(f, (m + i) % 4) for i in range(1, 4)]
    count = 64
    before = [((f + count - 1) % count, xh * 2 + core) for core in range(2)]
    after = [((f + 1) % count, xh * 2 + core) for core in range(2)]
    started = []
    numbers = {}

    def number(key):
        return numbers.setdefault(key, len(numbers))

    def remote(src, dst, key, device, keep=True):
        copy = pltpu.make_async_remote_copy(
            src_ref=src, dst_ref=dst, send_sem=send_sem.at[len(started) if keep else 0],
            recv_sem=recv_sem.at[key if not isinstance(key, tuple) else number(key)],
            device_id=device, device_id_type=MESH,
        )
        return copy

    def send(src, dst, key, device):
        copy = remote(src, dst, key, device)
        started.append(copy)
        copy.start()

    def received(dst, key):
        remote(dst, dst, key, twin, keep=False).wait_recv()

    locals_started = {}

    def load(src, dst, key, place):
        copy = pltpu.make_async_copy(src, dst, local_sem.at[place])
        copy.start()
        locals_started.setdefault(key, []).append(copy)

    barrier = pltpu.get_barrier_semaphore()
    passers = [(frame_of(y, z, 1 - xl), (1 - xh) * 2 + core) for core in range(2)]
    around = [((f + count + way * step) % count, xh * 2 + core)
              for way in (1, -1) for step in (1, 2) for core in range(2)]
    greeted = [twin, inner, *passers, *ring.values(), *group, *around]
    for device in greeted:
        pl.semaphore_signal(barrier, inc=1, device_id=device, device_id_type=MESH)

    half_columns = pl.multiple_of(c * INNER, INNER)
    other_columns = pl.multiple_of((1 - c) * INNER, INNER)
    own_rows = pl.multiple_of(c * ROWS, ROWS)
    buffers = [weights.at[r] for r in range(ROUNDS)] + [out_weights.at[r] for r in range(2)]
    load(mw_hbm, mod_weights, "mod", 0)
    load(x_hbm, own_x, "x", 1)
    load(x_hbm.at[:, pl.ds(half_columns, INNER)], half_x.at[pl.ds(own_rows, ROWS)], "half", 2)

    def slabs(r, core):
        if r < ROUNDS:
            for part in range(3):
                start = part * INNER + core * HALF + r * PAIR
                yield pl.ds(pl.multiple_of(start, PAIR), PAIR), pl.ds(part * PAIR, PAIR)
        else:
            start = core * INNER + (r - ROUNDS) * WIDE
            yield pl.ds(pl.multiple_of(start, WIDE), WIDE), pl.ds(0, WIDE)

    def source(r):
        return w_hbm if r < ROUNDS else wo_hbm

    def shard_rows(r, owner):
        return pl.ds(pl.multiple_of(owner * SHARD[r], SHARD[r]), SHARD[r])

    for r in range(5):
        for i, (here, there) in enumerate(slabs(r, c)):
            load(source(r).at[:, here], buffers[r].at[shard_rows(r, m), there], r, 3 + 3 * r + i)

    level = jnp.full((16, HEAD), levels[0], jnp.int32).astype(F32)
    sigma_now = flow_sigma((level + 1.0) / NOISE_LEVELS)
    step_size = sigma_now - flow_sigma(level / NOISE_LEVELS)
    index_row = lax.broadcasted_iota(jnp.int32, (16, HEAD), 1).astype(F32)
    angles = 1000.0 * sigma_now * jnp.exp(-math.log(10000.0) * index_row / HEAD)
    waves = [jax.nn.silu(wave(angles)).astype(BF16) for wave in (jnp.cos, jnp.sin)]
    for copy in locals_started.pop("mod"):
        copy.wait()
    columns_mod = jnp.dot(waves[0], mod_weights[:HEAD], preferred_element_type=F32)
    columns_mod += jnp.dot(waves[1], mod_weights[HEAD:], preferred_element_type=F32)
    part_mod[...] = columns_mod[:1]
    mod[m] = columns_mod[:1]
    pl.semaphore_wait(barrier, len(greeted))

    own = {"z": z, "y": y}
    length = {"z": NZ, "y": NY}
    missing = (1 - xh) * 2
    shard_of = {"a": missing + xl, "b": missing + 1 - xl}

    def piece(axis, owner, j, r):
        rows = PIECE[axis][r]
        start = owner * SHARD[r] + BASE[axis][r] + j * rows
        return buffers[r].at[pl.ds(pl.multiple_of(start, 16), rows)]

    fetched = []

    def direct(axis, r):
        return direct_key + 4 * r + 2 * (axis == "z")

    def fetch(r):
        first = len(started)

        def pieces():
            for axis in AXES[r]:
                rows = PIECE[axis][r]
                start = BASE[axis][r] + own[axis] * rows
                rows_here = pl.ds(pl.multiple_of(start, 16), rows)
                rows_there = pl.ds(pl.multiple_of(m * SHARD[r] + start, 16), rows)
                for core in range(2):
                    for here, there in slabs(r, core):
                        send(
                            source(r).at[rows_here, here], buffers[r].at[rows_there, there],
                            direct(axis, r) + jnp.where(c == 1 - xl, 0, 1), cross[core],
                        )

        if r in DIRECT:
            pieces()
            return
        pl.when(c == 1 - xl)(pieces)

        each = (len(started) - first) // len(AXES[r])
        for i in range(first, len(started)):
            rows = PIECE[AXES[r][(i - first) // each]][r]
            region = buffers[r].at[pl.ds(0, rows), pl.ds(0, PAIR if r < ROUNDS else WIDE)]
            started[i] = None
            fetched.append((region, i))

    def exchange(r):
        for here, there in slabs(r, 1 - c):
            send(
                source(r).at[:, here], buffers[r].at[shard_rows(r, m), there], ("twin", r), twin
            )

    def ring_send(axis, way, half, k, r):
        if k >= HOPS[axis, half, way]:
            return
        j = (own[axis] - way * k + length[axis]) % length[axis]
        region = piece(axis, shard_of[half], j, r)
        send(region, region, (axis, way, half, k + 1, r), ring[axis, way])

    def arrived(axis, way, half, k, r):
        j = (own[axis] - way * k + length[axis]) % length[axis]
        received(piece(axis, shard_of[half], j, r), (axis, way, half, k, r))

    def complete(r):
        for copy in locals_started.pop(r):
            copy.wait()
        received(buffers[r].at[shard_rows(r, xh * 2 + 1 - c)], ("twin", r))

    def next_send(i):
        core, part = i % 2, i // 2
        rows = ROWS // 2
        send(
            x_hbm.at[pl.ds(part * rows, rows), pl.ds(core * INNER, INNER)],
            next_x.at[pl.ds(pl.multiple_of(own_rows + part * rows, 16), rows)],
            next_x_key + c, before[core],
        )

    for device in group:
        send(part_mod, mod.at[m], mod_sem_key + m, device)
    fetch(0)
    fetch(1)
    send(
        x_hbm.at[:, pl.ds(other_columns, INNER)], half_x.at[pl.ds(own_rows, ROWS)], ("x",), twin
    )
    for r in range(5):
        exchange(r)
    fetch(2)
    for i in range(4):
        next_send(i)
    for i in range(1, 4):
        owner = (m + i) % 4
        received(mod.at[owner], mod_sem_key + owner)
    shift[:, :2304] = mod[0]
    shift[:, 2304:] = mod[1, :, :768]
    scale[:, :1536] = 1.0 + mod[1, :, 768:]
    scale[:, 1536:] = 1.0 + mod[2, :, :1536]
    gate[:, :768] = mod[2, :, 1536:]
    gate[:, 768:D] = mod[3]
    gate[:, D:] = step_size[:1]
    slot_before = (f + count - 1) % count
    send(gate, next_gate, ("gate",), (slot_before, m))
    for copy in locals_started.pop("x"):
        copy.wait()

    @pl.loop(0, ROWS // 16)
    def _(i):
        rows = own_x[pl.ds(pl.multiple_of(i * 16, 16), 16), :].astype(F32)
        center = jnp.mean(rows, axis=-1, keepdims=True)
        rows = rows - center
        spread = jnp.mean(rows * rows, axis=-1, keepdims=True)
        out = rows * lax.rsqrt(spread + 1e-06) * scale[...] + shift[...]
        hidden[pl.ds(pl.multiple_of(own_rows + i * 16, 16), 16), :] = out.astype(BF16)

    mine = hidden.at[pl.ds(own_rows, ROWS)]
    send(mine, mine, ("hidden",), twin)
    def halo_send(i):
        frame = hidden.at[pl.ds(pl.multiple_of(own_rows + i * SPATIAL, 16), SPATIAL)]
        passing = relay_rows.at[pl.ds(i * SPATIAL, SPATIAL)]
        device = (frame_of(y, z, 1 - xl), (1 - xh) * 2 + c)
        send(frame, passing, ("halo", i), device)

    sender = frame_of(y, z, 1 - xl)
    halo_frame = jnp.where(c == 1, sender + 1 - xh, sender + count - xh) % count
    halo_base = jnp.where(c == 1, CHIP, CHIP + ROWS)
    passed = []

    def relay(i):
        passing = relay_rows.at[pl.ds(i * SPATIAL, SPATIAL)]
        received(passing, ("halo", i))
        device = (halo_frame, xh * 2 + i)
        here = (halo_frame == f) & (c == i)
        region = hidden.at[pl.ds(pl.multiple_of(halo_base + i * SPATIAL, 16), SPATIAL)]
        place = len(started)
        started.append(None)
        passed.append((passing, here, place))

        @pl.when(here)
        def _():
            pltpu.make_async_copy(passing, region, recv_sem.at[halo_key + 1 - c]).start()

        @pl.when(jnp.logical_not(here))
        def _():
            pltpu.make_async_remote_copy(
                src_ref=passing, dst_ref=region, send_sem=send_sem.at[place],
                recv_sem=recv_sem.at[halo_key + 1 - c], device_id=device, device_id_type=MESH,
            ).start()

    def halo_forward():
        for side in range(2):
            region = hidden.at[
                pl.ds(pl.multiple_of(CHIP + side * ROWS + c * SPATIAL, 16), SPATIAL)
            ]
            received(region, halo_key + side)
            send(region, region, ("forward", side), twin)

    def halo_arrived():
        for side in range(2):
            region = hidden.at[
                pl.ds(pl.multiple_of(CHIP + side * ROWS + (1 - c) * SPATIAL, 16), SPATIAL)
            ]
            received(region, ("forward", side))

    def product(lo, r, part):
        return jnp.dot(
            hidden[lo : lo + CHIP, :], weights[r, :, part * PAIR : (part + 1) * PAIR],
            preferred_element_type=F32,
        )

    def normed(tile, gain):
        return tile * lax.rsqrt(jnp.mean(tile * tile, axis=-1, keepdims=True) + 1e-06) * gain

    def project(r, part, own_part):
        tile = product(0 if own_part else CHIP, r, part)
        for h in range(2):
            columns = slice(h * HEAD, (h + 1) * HEAD)
            head = tile[:, columns]
            if part == 0:
                head = normed(head, qgain[...] * (1.0 / math.sqrt(HEAD)))
            elif part == 1:
                head = normed(head, kgain[...])
            head = head.astype(BF16)
            if part == 0:
                queries[r, :, columns] = head
            else:
                target = keys if part == 1 else values
                if own_part:
                    target[r, ROWS : ROWS + CHIP, columns] = head
                else:
                    target[r, 0:ROWS, columns] = head[:ROWS]
                    target[r, ROWS + CHIP :, columns] = head[ROWS:]

    lane = lax.broadcasted_iota(jnp.int32, (1, WINDOW), 1)
    offset = sum((lane >= k * SPATIAL).astype(jnp.int32) for k in range(1, 5)) - REACH_LIMIT

    def attend(r):
        @pl.loop(0, 4)
        def _(i):
            q_rows = pl.ds(pl.multiple_of(i * SPATIAL, 16), SPATIAL)
            k_rows = pl.ds(pl.multiple_of(i * SPATIAL, 16), WINDOW)
            key_frame = f * 8 + xh * 4 + i + offset
            valid = (jnp.abs(offset) <= reach[0]) & (key_frame >= 0) & (key_frame < FRAMES)
            bias = jnp.where(valid, 0.0, -1e30)
            for h in range(2):
                columns = slice(h * HEAD, (h + 1) * HEAD)
                scores = lax.dot_general(
                    queries[r, q_rows, columns], keys[r, k_rows, columns],
                    (((1,), (1,)), ((), ())), preferred_element_type=F32,
                ) + bias
                peak = jnp.max(scores, axis=-1, keepdims=True)
                raised = jnp.exp(scores - peak)
                total = jnp.sum(raised, axis=-1, keepdims=True)
                out = jnp.dot(
                    raised.astype(BF16), values[r, k_rows, columns], preferred_element_type=F32
                )
                place = pl.multiple_of(c * HALF + r * PAIR + h * HEAD, HEAD)
                mixed[q_rows, pl.ds(place, HEAD)] = (out / total).astype(BF16)

        columns = pl.ds(pl.multiple_of(c * HALF + r * PAIR, PAIR), PAIR)
        send(mixed.at[:, columns], next_mixed.at[:, columns], ("next mixed", r), (slot_before, m))
        send(mixed.at[:, columns], mixed.at[:, columns], ("mixed", r), twin)

    def forward_mixed(r):
        region = next_mixed.at[:, pl.ds(pl.multiple_of(c * HALF + r * PAIR, PAIR), PAIR)]
        received(region, ("next mixed", r))
        send(region, region, ("forward mixed", r), twin)

    def all_mixed(buffer, name):
        for r in range(ROUNDS):
            columns = pl.ds(pl.multiple_of((1 - c) * HALF + r * PAIR, PAIR), PAIR)
            received(buffer.at[:, columns], (name, r))

    for i in range(2):
        halo_send(i)
    for r in range(3, 5):
        fetch(r)

    first = True
    for action in plan():
        kind, rest = action[0], action[1:]
        if kind == "wait":
            kind, rest = rest[0], rest[1:]
            if kind == "fetch":
                received(piece(rest[0], shard_of["a"], own[rest[0]], rest[1]), direct(*rest))
            elif kind == "swap":
                key = direct(*rest) + 1 if rest[1] in DIRECT else ("swap", *rest)
                received(piece(rest[0], shard_of["b"], own[rest[0]], rest[1]), key)
            elif kind == "ring":
                arrived(*rest)
            else:
                halo_forward()
        elif kind == "send":
            kind, rest = rest[0], rest[1:]
            if kind == "swap":
                region = piece(rest[0], shard_of["a"], own[rest[0]], rest[1])
                send(region, region, ("swap", *rest), inner)
            else:
                ring_send(*rest)
        elif kind == "relay":
            relay(*rest)
        elif kind == "complete":
            complete(*rest)
            if first:
                other = hidden.at[pl.ds(pl.multiple_of((1 - c) * ROWS, ROWS), ROWS)]
                received(other, ("hidden",))
                first = False
        elif kind == "project":
            project(*rest)
        elif kind == "attend":
            attend(*rest)
        else:
            halo_arrived()

    finals = []

    def finish(buffer, base_rows, gates, out, out_hbm, next_slot):
        for h in range(2):
            for t in range(3):
                lo = h * WIDE + t * PAIR
                attended = jnp.dot(
                    buffer[...], out_weights[h, :, t * PAIR : (t + 1) * PAIR],
                    preferred_element_type=F32,
                )
                gate_row = gates[:, pl.ds(pl.multiple_of(half_columns + lo, PAIR), PAIR)]
                rows = base_rows[:, lo : lo + PAIR].astype(F32)
                full = rows + gate_row * attended
                if next_slot:
                    step = jnp.concatenate([gates[:, D:]] * 2, axis=1)
                    full = rows - step * full
                out[:, lo : lo + PAIR] = full.astype(BF16)
            columns = pl.ds(pl.multiple_of(half_columns + h * WIDE, WIDE), WIDE)
            stage = pl.ds(h * WIDE, WIDE)
            twin_rows = pl.ds(pl.multiple_of((1 - c) * ROWS, ROWS), ROWS)
            send(
                out.at[twin_rows, stage], out_hbm.at[:, columns], ("out", next_slot, h), twin
            )
            copy = pltpu.make_async_copy(
                out.at[pl.ds(own_rows, ROWS), stage], out_hbm.at[:, columns],
                local_sem.at[18 + len(finals)],
            )
            copy.start()
            finals.append(copy)

    forward_mixed(0)
    complete(3)
    complete(4)
    for copy in locals_started.pop("half"):
        copy.wait()
    received(half_x.at[pl.ds(pl.multiple_of((1 - c) * ROWS, ROWS), ROWS)], ("x",))
    all_mixed(mixed, "mixed")
    finish(mixed, half_x, gate, vel, vel_hbm, False)
    forward_mixed(1)
    forward_mixed(2)
    received(next_gate, ("gate",))
    for core in range(2):
        received(next_x.at[pl.ds(core * ROWS, ROWS)], next_x_key + core)
    all_mixed(next_mixed, "forward mixed")
    finish(next_mixed, next_x, next_gate, stepped, next_hbm, True)
    for h in range(2):
        columns = pl.ds(pl.multiple_of(other_columns + h * WIDE, WIDE), WIDE)
        received(vel_hbm.at[:, columns], ("out", False, h))
        received(next_hbm.at[:, columns], ("out", True, h))
    for copy in finals:
        copy.wait()
    assert len(started) <= SENDS and len(numbers) <= mod_sem_key
    for copy in started:
        if copy is not None:
            copy.wait_send()

    for passing, here, place in passed:
        pl.when(jnp.logical_not(here))(
            pltpu.make_async_remote_copy(
                src_ref=passing, dst_ref=passing, send_sem=send_sem.at[place],
                recv_sem=recv_sem.at[0], device_id=twin, device_id_type=MESH,
            ).wait_send
        )

    @pl.when(c == 1 - xl)
    def _():
        for region, i in fetched:
            pltpu.make_async_remote_copy(
                src_ref=region, dst_ref=region, send_sem=send_sem.at[i], recv_sem=recv_sem.at[0],
                device_id=twin, device_id_type=MESH,
            ).wait_send()


mod_sem_key = 160
halo_key = 164
next_x_key = 166
direct_key = 168
SEMAPHORES = 188
SENDS = 288


def per_device(
    latents, levels, window_reach, query_gain, key_gain, qkv_weight, out_weight, mod_weight
):
    vmem = pl.BlockSpec(memory_space=pltpu.VMEM)
    smem = pl.BlockSpec(memory_space=pltpu.SMEM)
    hbm = pl.BlockSpec(memory_space=pl.ANY)
    shape = jax.ShapeDtypeStruct((ROWS, D), BF16)
    velocity, queue_next = pl.pallas_call(
        kernel,
        out_shape=(shape, shape),
        in_specs=[hbm, hbm, hbm, hbm, smem, smem, vmem, vmem],
        out_specs=(hbm, hbm),
        scratch_shapes=[
            pltpu.VMEM((ROUNDS, D, WIDE), BF16),
            pltpu.VMEM((2, INNER, WIDE), BF16),
            pltpu.VMEM((2 * CHIP, D), BF16),
            pltpu.VMEM((ROWS, D), BF16),
            pltpu.VMEM((CHIP, INNER), BF16),
            pltpu.VMEM((CHIP, INNER), BF16),
            pltpu.VMEM((FREQ, 2304), BF16),
            pltpu.VMEM((1, 2304), F32),
            pltpu.VMEM((4, 1, 2304), F32),
            pltpu.VMEM((1, D), F32),
            pltpu.VMEM((1, D), F32),
            pltpu.VMEM((1, D + HEAD), F32),
            pltpu.VMEM((1, D + HEAD), F32),
            pltpu.VMEM((ROWS, D), BF16),
            pltpu.VMEM((ROUNDS, CHIP, PAIR), BF16),
            pltpu.VMEM((ROUNDS, 2 * CHIP, PAIR), BF16),
            pltpu.VMEM((ROUNDS, 2 * CHIP, PAIR), BF16),
            pltpu.VMEM((CHIP, INNER), BF16),
            pltpu.VMEM((CHIP, INNER), BF16),
            pltpu.VMEM((CHIP, INNER), BF16),
            pltpu.VMEM((CHIP, INNER), BF16),
            pltpu.SemaphoreType.DMA((SENDS,)),
            pltpu.SemaphoreType.DMA((SEMAPHORES,)),
            pltpu.SemaphoreType.DMA((24,)),
        ],
        compiler_params=pltpu.CompilerParams(
            collective_id=0, has_side_effects=True, vmem_limit_bytes=56 * 2**20
        ),
    )(
        latents.reshape(ROWS, D), qkv_weight, out_weight, mod_weight, levels, window_reach,
        query_gain.reshape(1, HEAD), key_gain.reshape(1, HEAD),
    )
    return (queue_next.reshape(2, SPATIAL, D), velocity.reshape(2, SPATIAL, D))


def solution(mesh):
    return jax.shard_map(
        per_device,
        mesh=mesh,
        in_specs=(
            P(("frame", "mp"), None, None),
            P("frame"),
            P("frame"),
            P(),
            P(),
            P("mp", None),
            P("mp", None),
            P(None, "mp"),
        ),
        out_specs=(P(("frame", "mp"), None, None), P(("frame", "mp"), None, None)),
        check_vma=False,
    )
```
